128 devices in a mesh: section: 2 (over z_lo), expert: 16 (over x, y), shard: 4 (over z_hi, core).
Axes of the slice: x: 4, y: 4, z: 4 (z_hi: 2, z_lo: 2; z = z_hi * 2 + z_lo), core: 2. Of those that a mesh axis runs over, the one named last changes fastest.
Arguments:
- images: bfloat16 [2, 256, 50, 512], P(None, ('expert', 'shard')), may hold values from -6 to 6
- cotangent: bfloat16 [2, 256, 50, 512], P(None, ('expert', 'shard')), may hold values from -6 to 6
- ln1_gain: bfloat16 [2, 512], P('section', 'shard'), may hold values from 0.5 to 1.5
- qkv_weight: bfloat16 [2, 512, 1536], P('section', 'shard'), may hold values from -0.25 to 0.25
- out_weight: bfloat16 [2, 512, 512], P('section', 'shard'), may hold values from -0.75 to 0.75
- ln2_gain: bfloat16 [2, 512], P('section', 'shard'), may hold values from 0.5 to 1.5
- router_weight: bfloat16 [2, 512, 32], P('section', 'shard'), may hold values from -0.1875 to 0.1875
- up_weight: bfloat16 [2, 32, 2048, 512], P('section', 'expert', 'shard'), may hold values from -0.25 to 0.25
- down_weight: bfloat16 [2, 32, 2048, 512], P('section', 'expert', 'shard'), may hold values from -0.25 to 0.25
- routes: int32 [2, 2, 256, 50, 2], P('section', None, ('expert', 'shard')), may hold values from 0 to 31, all different within a row; in each aligned block of 200 rows (0 to 199, 200 to 399, ..., all dimensions but the last counted through in order) at most 14 rows name the same one
Outputs:
- layer_out: bfloat16 [2, 2, 256, 50, 512], P('section', None, ('expert', 'shard'))
- layer_in_grad: bfloat16 [2, 2, 256, 50, 512], P('section', None, ('expert', 'shard'))
- ln1_gain_grad: float32 [2, 512], P('section', 'shard')
- qkv_weight_grad: float32 [2, 512, 1536], P('section', 'shard')
- out_weight_grad: float32 [2, 512, 512], P('section', 'shard')
- ln2_gain_grad: float32 [2, 512], P('section', 'shard')
- router_weight_grad: float32 [2, 512, 32], P('section', 'shard')
- up_weight_grad: float32 [2, 32, 2048, 512], P('section', 'expert', 'shard')
- down_weight_grad: float32 [2, 32, 2048, 512], P('section', 'expert', 'shard')
The draws below stay inside these ranges and needn't reach their ends.
Inputs may be any that keep to these rules, and one draw needn't show every extreme that they name: `routes`: in each aligned block of 200 tokens (the tokens of one device in one micro-batch of one layer) no expert is named by more than 14 tokens, a bound that some block reaches; the 2 experts of a token differ.
All inputs are finite; a program needn't handle non-finite values.
Results may differ from the reference program's by a relative error of at most 0.03.
Values may be sent and summed in bfloat16 or wider, within the bound.
A program may use at most 128 MiB of HBM per device.

```python
import math
import jax
import jax.numpy as jnp
import numpy as np
from jax import lax

D = 512
HEADS = 8
HEAD_DIM = 64
FF = 2048
TOPK = 2
SEQ = 50
IMG_DEV = 4
MICRO = 2
LAYERS = 2
EXPERTS = 32
IMGS = 256
CAP = 14


def levels(rng, dims, shards, least, high):
    level, own = 1.0, jax.random.fold_in(rng, 6)
    for dim, blocks in shards:
        heights = jnp.exp(jax.random.uniform(jax.random.fold_in(own, dim), (blocks,), jnp.float32, least / len(shards), high / len(shards)))
        level = level * jnp.repeat(heights, dims[dim] // blocks).reshape([-1 if axis == dim else 1 for axis in range(len(dims))])
    return level


def assign_block(own_key, own, number, rows, number_of, top, bound, skew):
    sequence = jax.random.permutation(own_key, number_of)
    crowded, usual = shares(number_of, rows * top, bound, skew, True), shares(number_of, rows * top, bound, skew, False)
    places = jnp.arange(number_of)

    def named(tallies, turn):
        used = int((tallies > 0).sum())
        fixed = max(1, used // 4)
        moved = fixed + (places - fixed + turn * (used - fixed)) % max(1, number_of - fixed)
        return jnp.zeros((number_of,), jnp.int32).at[sequence[jnp.where(places < fixed, places, moved)]].set(jnp.asarray(tallies, jnp.int32))

    tallies = jnp.where(number % 4 == 0, named(crowded, number // 4), named(usual, number - number // 4 - 1))
    mixed = jax.random.permutation(jax.random.fold_in(own, 3), number_of)
    giver, receiver = mixed[0:number_of // 2 * 2:2], mixed[1:number_of // 2 * 2:2]
    slack = jnp.minimum(tallies[giver] - 1, bound - tallies[receiver]) // 2
    slack = jnp.where((giver == sequence[0]) | (receiver == sequence[0]) | (tallies[receiver] == 0), 0, jnp.maximum(slack, 0))
    moved = jax.random.randint(jax.random.fold_in(own, 4), (number_of // 2,), 0, 1 << 20) % (slack + 1)
    tallies = tallies.at[giver].add(-moved).at[receiver].add(moved)
    labels = jnp.searchsorted(jnp.cumsum(tallies), jnp.arange(rows * top), side="right").astype(jnp.int32)
    listing = labels.reshape(top, rows).T
    listing = listing[jax.random.permutation(jax.random.fold_in(own, 1), rows)]
    turn = jax.random.randint(jax.random.fold_in(own, 2), (rows, 1), 0, top)
    return jnp.take_along_axis(listing, (jnp.arange(top)[None, :] + turn) % top, axis=1)


def shares(count, total, limit, skew, full):
    loads = [(1 << 20) // math.isqrt(grade ** skew) + 1 for grade in range(1, count + 1)]
    largest = limit if full else min(limit, max(-(-total // count), total * loads[0] // sum(loads)))
    least = 1 if total - largest >= count - 1 else 0
    holding, surplus = [largest] + [least] * (count - 1), total - largest - least * (count - 1)
    while surplus > 0:
        free = [i for i in range(1, count) if holding[i] < largest] or [i for i in range(1, count) if holding[i] < limit]
        whole, remaining = sum([loads[i] for i in free]), surplus
        for i in free:
            more = min(limit - holding[i], max(1, remaining * loads[i] // whole), surplus)
            holding[i] = holding[i] + more
            surplus = surplus - more
    return np.array(holding)


def normal_values(rng, extent, scale, reach, split=(), kind=jnp.bfloat16):
    result = jax.random.normal(rng, extent, jnp.float32) * scale
    if len(split) > 0:
        result = levels(rng, extent, split, -0.22, 0.18) * result
    return jnp.clip(result, min=-reach, max=reach).astype(kind)


def setup_inputs(seed: int = 0) -> dict:
    seeds = jax.random.split(jax.random.key(seed), 11)
    images = normal_values(seeds[0], (MICRO, IMGS, SEQ, D), 1.0, 6.0, ((1, 64),))
    cotangent = normal_values(seeds[1], (MICRO, IMGS, SEQ, D), 1.0, 6.0, ((1, 64),))
    ln1_gain = jnp.clip(1.0 + 0.1 * jax.random.normal(seeds[2], (LAYERS, D), jnp.float32), 0.5, 1.5).astype(jnp.bfloat16)
    qkv_weight = normal_values(seeds[3], (LAYERS, D, 3 * D), D ** -0.5, 0.25, ((0, 2), (1, 4)))
    out_weight = normal_values(seeds[4], (LAYERS, D, D), (D // 8) ** -0.5, 0.75, ((0, 2), (1, 4)))
    ln2_gain = jnp.clip(1.0 + 0.1 * jax.random.normal(seeds[5], (LAYERS, D), jnp.float32), 0.5, 1.5).astype(jnp.bfloat16)
    router_weight = normal_values(seeds[6], (LAYERS, D, EXPERTS), (2 * D) ** -0.5, 0.1875, ((0, 2), (1, 4)))
    up_weight = normal_values(seeds[7], (LAYERS, EXPERTS, FF, D), D ** -0.5, 0.25, ((0, 2), (1, 16), (2, 4)))
    down_weight = normal_values(seeds[8], (LAYERS, EXPERTS, FF, D), (FF // 4) ** -0.5, 0.25, ((0, 2), (1, 16), (2, 4)))
    routes_keys = jax.random.split(jax.random.fold_in(seeds[9], 1), LAYERS * MICRO * IMGS * SEQ // (IMG_DEV * SEQ))
    routes_turns = jax.random.permutation(jax.random.fold_in(seeds[9], 3), LAYERS * MICRO * IMGS * SEQ // (IMG_DEV * SEQ))
    routes = jax.vmap(lambda own, number: assign_block(jax.random.fold_in(seeds[9], 2), own, number, IMG_DEV * SEQ, EXPERTS, TOPK, CAP, 1))(routes_keys, routes_turns).reshape((LAYERS, MICRO, IMGS, SEQ, TOPK))
    return {"images": images, "cotangent": cotangent, "ln1_gain": ln1_gain, "qkv_weight": qkv_weight, "out_weight": out_weight, "ln2_gain": ln2_gain, "router_weight": router_weight, "up_weight": up_weight, "down_weight": down_weight, "routes": routes}


@jax.custom_vjp
def low(v):
    return lax.optimization_barrier(v.astype(jnp.bfloat16)).astype(jnp.float32)

@jax.custom_vjp
def low_back(v):
    return v

def low_keep(v):
    return (low(v), None)

def low_pass(kept, grad):
    return (grad,)

def back_keep(v):
    return (v, None)

def back_low(kept, grad):
    return (low(grad),)
low.defvjp(low_keep, low_pass)
low_back.defvjp(back_keep, back_low)
epsilon = 1e-06
highest = lax.Precision.HIGHEST

def normalize(values, gain):
    center = lax.optimization_barrier(jnp.mean(values, axis=-1, keepdims=True))
    shifted = values - center
    spread = lax.optimization_barrier(jnp.mean(shifted * shifted, axis=-1, keepdims=True))
    return shifted * lax.rsqrt(spread + epsilon) * gain

def slot_targets(route_block):
    blocks = IMGS // IMG_DEV
    flat_routes = route_block.reshape(blocks, IMG_DEV * SEQ * TOPK).astype(jnp.int32)
    choose = (flat_routes[:, :, None] == jnp.arange(EXPERTS, dtype=jnp.int32)).astype(jnp.int32)
    earlier = jnp.cumsum(choose, axis=1) - choose
    slot_index = lax.optimization_barrier(jnp.sum(earlier * choose, axis=2))
    block_index = jnp.arange(blocks, dtype=jnp.int32)[:, None]
    return ((flat_routes * blocks + block_index) * CAP + slot_index).reshape(-1).astype(jnp.int32)

def layer(inputs, route_block, gain_one, weight_qkv, weight_out, gain_two, weight_router, weight_up, weight_down):
    tokens = IMGS * SEQ
    scaling = HEAD_DIM ** (-0.5)
    rows_in = inputs.reshape(tokens, D)
    first_in = low(normalize(rows_in, gain_one))
    mixed_qkv = low_back(low(jnp.dot(first_in, weight_qkv, precision=highest)))
    mixed_qkv = mixed_qkv.reshape(IMGS, SEQ, 3, HEADS, HEAD_DIM)
    scores = low_back(jnp.einsum('bqhd,bkhd->bhqk', mixed_qkv[:, :, 0], mixed_qkv[:, :, 1], precision=highest) * scaling)
    probability = low(jax.nn.softmax(scores, axis=-1))
    attended = low_back(low(jnp.einsum('bhqk,bkhd->bqhd', probability, mixed_qkv[:, :, 2], precision=highest)))
    hidden = rows_in + low_back(jnp.dot(attended.reshape(tokens, D), weight_out, precision=highest))
    second_in = low(normalize(hidden, gain_two))
    logits = low_back(jnp.dot(second_in, weight_router, precision=highest))
    flat_routes = route_block.reshape(tokens, TOPK)
    choose = (flat_routes[:, :, None] == jnp.arange(EXPERTS, dtype=jnp.int32)).astype(jnp.float32)
    gate_values = jax.nn.softmax(lax.optimization_barrier(jnp.sum(choose * logits[:, None, :], axis=-1)), axis=-1)
    copies = low_back(jnp.broadcast_to(second_in[:, None, :], (tokens, TOPK, D))).reshape(tokens * TOPK, D)
    targets = slot_targets(route_block)
    buffer = jnp.zeros((EXPERTS * (IMGS // IMG_DEV) * CAP, D), jnp.float32).at[targets].add(copies)
    buffer = buffer.reshape(EXPERTS, IMGS // IMG_DEV * CAP, D)
    before = low_back(jnp.einsum('erd,efd->erf', buffer, weight_up, precision=highest))
    active = low(jax.nn.gelu(before))
    returned = low_back(low(jnp.einsum('erf,efd->erd', active, weight_down, precision=highest)))
    picked = returned.reshape(-1, D)[targets].reshape(tokens, TOPK, D)
    return (hidden + lax.optimization_barrier(jnp.sum(gate_values[:, :, None] * picked, axis=1))).reshape(IMGS, SEQ, D)

def reference(images, cotangent, ln1_gain, qkv_weight, out_weight, ln2_gain, router_weight, up_weight, down_weight, routes):
    weights = tuple((item.astype(jnp.float32) for item in (ln1_gain, qkv_weight, out_weight, ln2_gain, router_weight, up_weight, down_weight)))
    inputs = images.astype(jnp.float32)
    probe = jnp.zeros(inputs.shape, jnp.float32)
    stepper = jax.checkpoint(layer)

    def forward(weights, inputs, probe):
        firsts = []
        seconds = []
        for micro in range(MICRO):
            first = low(stepper(inputs[micro], routes[0, micro], *[item[0] for item in weights]))
            joined = low_back(first + probe[micro])
            seconds.append(stepper(joined, routes[1, micro], *[item[1] for item in weights]))
            firsts.append(first)
        return (jnp.stack(firsts), jnp.stack(seconds))
    outputs, pullback = jax.vjp(forward, weights, inputs, probe)
    weight_grads, input_grad, probe_grad = pullback((jnp.zeros_like(outputs[0]), cotangent.astype(jnp.float32)))
    layer_out = jnp.stack([outputs[0], outputs[1]]).astype(jnp.bfloat16)
    layer_in_grad = jnp.stack([input_grad, probe_grad]).astype(jnp.bfloat16)
    return (layer_out, layer_in_grad, weight_grads[0], weight_grads[1], weight_grads[2], weight_grads[3], weight_grads[4], weight_grads[5], weight_grads[6])
```

```python
import jax
import jax.numpy as jnp
from jax import lax
from jax.experimental import pallas as pl
from jax.experimental.pallas import tpu as pltpu
from jax.sharding import PartitionSpec as P

HEADS = 8
HEAD_DIM = 64
TOPK = 2
SEQ = 50
ROWS = 200
T = 256
D = 512
EXPERTS = 32
SLOTS = 16
SHARED = 2176
WIDE = 1152
EPS = 1e-06
F32 = jnp.float32
BF16 = jnp.bfloat16
MESH = pl.DeviceIdType.MESH


def nn(a, b):
    return lax.dot_general(a, b, (((1,), (0,)), ((), ())), preferred_element_type=F32)


def nt(a, b):
    return lax.dot_general(a, b, (((1,), (1,)), ((), ())), preferred_element_type=F32)


def tn(a, b):
    return lax.dot_general(a, b, (((0,), (0,)), ((), ())), preferred_element_type=F32)


def iota(shape, dim):
    return lax.broadcasted_iota(jnp.int32, shape, dim).astype(F32)


def one(condition):
    return jnp.where(condition, 1.0, 0.0)


def normalize(values):
    shifted = values - jnp.mean(values, axis=-1, keepdims=True)
    inverse = lax.rsqrt(jnp.mean(shifted * shifted, axis=-1, keepdims=True) + EPS)
    return shifted * inverse, inverse


def norm_back(grad, normed, inverse):
    mean_grad = jnp.mean(grad, axis=-1, keepdims=True)
    mean_cross = jnp.mean(grad * normed, axis=-1, keepdims=True)
    return inverse * (grad - mean_grad - normed * mean_cross)


ROOT = 0.7978845608028654
CUBE = 0.044715


def gelu(x):
    return 0.5 * x * (1.0 + jnp.tanh(ROOT * (x + CUBE * x * x * x)))


def gelu_both(x):
    square = x * x
    bent = jnp.tanh(ROOT * x * (1.0 + CUBE * square))
    half = 0.5 * (1.0 + bent)
    slope = half + 0.5 * x * (1.0 - bent * bent) * (ROOT * (1.0 + 3.0 * CUBE * square))
    return x * half, slope


A2A_S, A2A_R = 0, 8
ROUTE_S, ROUTE_R = 16, 17
SH_S, SH_R, SHF_S, SHF_R = 18, 19, 21, 23
W_S, W_R, WF_S, WF_R = 25, 26, 28, 30
GWA_S, GWA_R, GWB_S, GWB_R = 32, 34, 36, 40
GSA_S, GSA_R, GSB_S, GSB_R = 41, 43, 45, 47
GSC_S, GSC_R, GSD_S, GSD_R = 49, 53, 54, 55
LO_S, LO_R, LI_S, LI_R = 56, 57, 58, 59
SEMS = 60


def kernel(
    x, cot, rt, shp, up, dn,
    lout, lig, ebuf, gd,
    w, sh, rts, rcol, bias, d_t, p_t,
    qkv_s, o_s, hid, pick, gat,
    rows_b, ret_b, g_b, dr_b, sbuf, acc,
    act_t, gp_t, dp_t, dqkv,
    gw, gwa, gs, gsa, gsb, gsc_s, gsc, gd_s, lo, li, sem,
):
    s, e, h = lax.axis_index("section"), lax.axis_index("expert"), lax.axis_index("shard")
    zh, c = lax.div(h, 2), lax.rem(h, 2)
    me = e * 2 + s
    sibling = (s, e, 2 * zh + 1 - c)
    other = (1 - s, e, h)

    def put(src, dst, send, recv, device):
        pltpu.make_async_remote_copy(
            src_ref=src, dst_ref=dst, send_sem=sem.at[send], recv_sem=sem.at[recv],
            device_id=device, device_id_type=MESH,
        ).start()

    def local(src, dst, recv):
        pltpu.make_async_copy(src, dst, sem.at[recv]).start()

    def wait(ref, number):
        pltpu.make_async_copy(ref, ref, sem.at[number]).wait()

    def put_or_local(own, src, dst, send, recv, device, here=None):
        @pl.when(own)
        def _():
            local(src, dst, recv if here is None else here)

        @pl.when(jnp.logical_not(own))
        def _():
            put(src, dst, send, recv, device)

    def wait_unless(own, ref, number):
        @pl.when(jnp.logical_not(own))
        def _():
            wait(ref, number)

    def a2a_start(phase, dst):
        local(sbuf.at[me], dst.at[me], A2A_R + phase)

        def step(i, carry):
            t = lax.rem(me + i, EXPERTS)
            put(sbuf.at[t], dst.at[me], A2A_S + phase, A2A_R + phase,
                (lax.rem(t, 2), lax.div(t, 2), h))
            return carry

        lax.fori_loop(1, EXPERTS, step, 0)

    def a2a_finish(phase, dst):
        wait(dst, A2A_R + phase)
        wait(sbuf.at[pl.ds(0, EXPERTS - 1)], A2A_S + phase)

    put(rt.at[1 - s], rts.at[s], ROUTE_S, ROUTE_R, other)
    rts[s] = rt[s]
    for layer in range(2):
        @pl.when(s == layer)
        def _():
            for to_s in range(2):
                for to_zh in range(2):
                    put_or_local(
                        jnp.logical_and(s == to_s, zh == to_zh),
                        shp, sh.at[layer, pl.ds(pl.multiple_of(h * 128, 128), 128)],
                        SH_S, SH_R + layer, (to_s, e, 2 * to_zh + c),
                    )

    def weights_start(layer):
        @pl.when(s == layer)
        def _():
            for to_s in range(2):
                for to_zh in range(2):
                    own = jnp.logical_and(s == to_s, zh == to_zh)
                    device = (to_s, e, 2 * to_zh + c)
                    put_or_local(own, up.at[to_s], w.at[layer, h, 0], W_S, W_R + layer, device)
                    put_or_local(own, dn.at[to_s], w.at[layer, h, 1], W_S, W_R + layer, device)

    weights_start(0)

    def image_of(index):
        return one(index >= 50) + one(index >= 100) + one(index >= 150) + one(index >= 200)

    bias[...] = jnp.where(
        image_of(iota((T, T), 0)) == image_of(iota((T, T), 1)), 0.0, -1e30
    )
    lane = iota((T, 128), 1)
    first_half = lane < 64.0
    half_row = iota((1, 128), 1)
    halves = (one(half_row < 64.0).astype(BF16), one(half_row >= 64.0).astype(BF16))
    sel_row, sel_lane = iota((8, 128), 0), iota((8, 128), 1)
    select = one(sel_lane == sel_row + 32.0) * one(sel_row < 2.0)
    select = select.astype(BF16)

    wait(rts.at[0], ROUTE_R)
    wait(rts.at[0], ROUTE_S)
    upper = one(iota((T, T), 0) < iota((T, T), 1)).astype(BF16)
    eye = one(sel_lane == sel_row).astype(BF16)
    for l in range(2):
        route = rts[l]
        number = iota((EXPERTS, T), 0)
        chosen = [one(route[k:k + 1] == number) for k in range(2)]
        earlier = nn((chosen[0] + chosen[1]).astype(BF16), upper)
        slot = [jnp.sum(earlier * chosen[k], axis=0, keepdims=True) for k in range(2)]
        slot_number = iota((EXPERTS * SLOTS, T), 0)
        for k in range(2):
            d_t[l, k] = one(slot_number == route[k:k + 1] * SLOTS + slot[k]).astype(BF16)
        row8 = iota((8, T), 0)
        listing = jnp.where(
            row8 == 0.0, route[0:1],
            jnp.where(row8 == 1.0, route[1:2],
                      jnp.where(row8 == 2.0, slot[0], jnp.where(row8 == 3.0, slot[1], 0.0))),
        )
        columns = tn(listing.astype(BF16), eye)
        rcol[l] = columns
        lane_number = iota((T, EXPERTS * SLOTS), 1)
        for k in range(2):
            target = columns[:, k:k + 1] * SLOTS + columns[:, 2 + k:3 + k]
            p_t[l, k] = one(lane_number == target).astype(BF16)

    def choices(l):
        columns = rcol[l]
        return [one(lane == columns[:, k:k + 1]) for k in range(2)]

    def gains(l):
        rows = nt(select, sh[l, :, 2048:2176])
        return rows[0:1], rows[1:2]

    def shared_forward(l):
        wait(sh.at[l, pl.ds(0, 256)], SH_R + l)
        for from_zh in range(2):
            part = sh.at[l, pl.ds(pl.multiple_of((2 * from_zh + c) * 128, 128), 128)]
            put(part, part, SHF_S + l, SHF_R + l, sibling)
        wait(sh.at[l, pl.ds(0, 256)], SHF_R + l)
        wait(sh.at[l, pl.ds(0, 256)], SHF_S + l)

    def weights_forward(l):
        wait(w.at[l, pl.ds(0, 2)], W_R + l)
        for from_zh in range(2):
            part = w.at[l, 2 * from_zh + c]
            put(part, part, WF_S + l, WF_R + l, sibling)

    def weights_finish(l):
        for number in (WF_R + l, WF_S + l):
            wait(w.at[l, pl.ds(0, 2)], number)

    def forward(l):
        rows_in = (x[...] if l == 0 else lo[0]).astype(F32)
        normed, _ = normalize(rows_in)
        shared_forward(l)
        gain_one, gain_two = gains(l)
        first_in = (normed * gain_one).astype(BF16)
        qkv_s[l] = nn(first_in, sh[l, :, 0:1536]).astype(BF16)
        for pair in range(4):
            at = pair * 128
            q = qkv_s[l, :, at:at + 128]
            k = qkv_s[l, :, 512 + at:640 + at]
            v = qkv_s[l, :, 1024 + at:1152 + at]
            outs = []
            for half in range(2):
                scores = nt(q * halves[half], k) * (HEAD_DIM ** -0.5) + bias[...]
                raised = jnp.exp(scores - jnp.max(scores, axis=-1, keepdims=True))
                chance = raised / jnp.sum(raised, axis=-1, keepdims=True)
                outs.append(nn(chance.astype(BF16), v))
            o_s[l, :, at:at + 128] = jnp.where(first_half, outs[0], outs[1]).astype(BF16)
        hidden = rows_in + nn(o_s[l], sh[l, :, 1536:2048])
        hid[l] = hidden
        normed, _ = normalize(hidden)
        second_in = (normed * gain_two).astype(BF16)
        sbuf[...] = nn(d_t[l, 0] + d_t[l, 1], second_in).astype(BF16).reshape(EXPERTS, SLOTS, D)
        a2a_start(2 * l, rows_b.at[l])
        logits = nn(second_in, sh[l, :, 2048:2176])
        picked = [jnp.sum(ch * logits, axis=1, keepdims=True) for ch in choices(l)]
        top = jnp.maximum(picked[0], picked[1])
        raised = [jnp.exp(value - top) for value in picked]
        total = raised[0] + raised[1]
        gate = [value / total for value in raised]
        gat[l] = jnp.where(lane == 0.0, gate[0], jnp.where(lane == 1.0, gate[1], 0.0))
        weights_forward(l)
        a2a_finish(2 * l, rows_b.at[l])
        weights_finish(l)
        acc[...] = jnp.zeros_like(acc)

        def piece(j, carry):
            before = nt(rows_b[l].reshape(EXPERTS * SLOTS, D), w[l, j, 0])
            acc[...] += nn(gelu(before).astype(BF16), w[l, j, 1])
            return carry

        lax.fori_loop(0, 4, piece, 0)
        sbuf[...] = acc[...].astype(BF16).reshape(EXPERTS, SLOTS, D)
        a2a_start(2 * l + 1, ret_b.at[l])
        a2a_finish(2 * l + 1, ret_b.at[l])
        returned = ret_b[l].reshape(EXPERTS * SLOTS, D)
        result = hid[l]
        for k in range(2):
            mine = nn(p_t[l, k], returned)
            pick[l, k] = mine.astype(BF16)
            result = result + gat[l, :, k:k + 1] * mine
        lo[l] = result.astype(BF16)

    def gw_a(l):
        for to_zh in range(2):
            put(gw.at[2 * to_zh + 1 - c], gwa.at[l, to_zh], GWA_S + l, GWA_R + l, sibling)

    def gw_b(l):
        wait(gwa.at[l], GWA_R + l)
        for to_zh in range(2):
            j = 2 * to_zh + c
            own = jnp.logical_and(s == l, zh == to_zh)
            gw[j] = (gw[j].astype(F32) + gwa[l, to_zh].astype(F32)).astype(BF16)
            send = GWB_S + 2 * l + to_zh
            put_or_local(own, gw.at[j], ebuf.at[2 * s + zh], send, GWB_R, (l, e, j), send)

    def gw_sent(l):
        wait(gwa.at[l], GWA_S + l)
        for to_zh in range(2):
            wait(gw.at[0], GWB_S + 2 * l + to_zh)

    def gs_a(l):
        for to_zh in range(2):
            put(gs.at[l, 2 * to_zh + 1 - c], gsa.at[l, to_zh], GSA_S + l, GSA_R + l, sibling)

    def peers(step):
        def body(i, carry):
            step(lax.rem(e + i, 16))
            return carry

        lax.fori_loop(1, 16, body, 0)

    def gs_b(l):
        wait(gsa.at[l], GSA_R + l)
        for to_zh in range(2):
            j = 2 * to_zh + c
            gs[l, j] = (gs[l, j].astype(F32) + gsa[l, to_zh].astype(F32)).astype(BF16)

        def part(to_zh, to_e):
            return gs.at[l, 2 * to_zh + c, pl.ds(pl.multiple_of(to_e * 16, 16), 16)]

        def step(to_e):
            for to_zh in range(2):
                put(part(to_zh, to_e), gsb.at[l, e, to_zh], GSB_S + l, GSB_R + l, (s, to_e, h))

        for to_zh in range(2):
            local(part(to_zh, e), gsb.at[l, e, to_zh], GSB_R + l)
        peers(step)

    def gs_c(l):
        wait(gsb.at[l], GSB_R + l)
        total = gsb[l, 0].astype(F32)
        for source in range(1, 16):
            total = total + gsb[l, source].astype(F32)
        gsc_s[l] = total.astype(BF16)
        for to_zh in range(2):
            own = jnp.logical_and(s == l, zh == to_zh)
            put_or_local(own, gsc_s.at[l, to_zh], gsc.at[2 * s + zh], GSC_S + 2 * l + to_zh, GSC_R,
                         (l, e, 2 * to_zh + c))

    def gs_d():
        wait(gsc, GSC_R)
        total = gsc[0].astype(F32)
        for source in range(1, 4):
            total = total + gsc[source].astype(F32)
        gd_s[...] = total.astype(BF16)
        local(gd_s, gd.at[e], GSD_R)
        peers(lambda to_e: put(gd_s, gd.at[e], GSD_S, GSD_R, (s, to_e, h)))

    def gs_sent(l):
        wait(gsa.at[l], GSA_S + l)
        wait(gsb.at[l, pl.ds(0, 15)], GSB_S + l)
        for to_zh in range(2):
            wait_unless(jnp.logical_and(s == l, zh == to_zh), gsc_s.at[l, to_zh], GSC_S + 2 * l + to_zh)

    def backward(l, grad_out, hook_one, hook_two):
        gate = [gat[l, :, k:k + 1] for k in range(2)]
        grad_gate = [
            jnp.sum(grad_out * pick[l, k].astype(F32), axis=-1, keepdims=True) for k in range(2)
        ]
        copies = [(gate[k] * grad_out).astype(BF16) for k in range(2)]
        sent = nn(d_t[l, 0], copies[0]) + nn(d_t[l, 1], copies[1])
        sbuf[...] = sent.astype(BF16).reshape(EXPERTS, SLOTS, D)
        a2a_start(4 + 2 * l, g_b.at[l])

        def again(j, carry):
            before = nt(w[l, j, 0], rows_b[l].reshape(EXPERTS * SLOTS, D))
            active, slope = gelu_both(before)
            act_t[j] = active.astype(BF16)
            gp_t[j] = slope
            return carry

        lax.fori_loop(0, 4, again, 0)
        hook_one()
        a2a_finish(4 + 2 * l, g_b.at[l])
        acc[...] = jnp.zeros_like(acc)

        def back(j, carry):
            grad_active = nt(w[l, j, 1], g_b[l].reshape(EXPERTS * SLOTS, D))
            grad_before = (grad_active * gp_t[j]).astype(BF16)
            dp_t[j] = grad_before
            acc[...] += tn(grad_before, w[l, j, 0])
            return carry

        lax.fori_loop(0, 4, back, 0)
        sbuf[...] = acc[...].astype(BF16).reshape(EXPERTS, SLOTS, D)
        a2a_start(5 + 2 * l, dr_b.at[l])

        def weight_grads(j, carry):
            gw[j, 1] = nn(act_t[j], g_b[l].reshape(EXPERTS * SLOTS, D)).astype(BF16)
            gw[j, 0] = nn(dp_t[j], rows_b[l].reshape(EXPERTS * SLOTS, D)).astype(BF16)
            return carry

        lax.fori_loop(0, 4, weight_grads, 0)
        gw_a(l)
        total = gate[0] * grad_gate[0] + gate[1] * grad_gate[1]
        chosen = choices(l)
        grad_logits = (
            chosen[0] * (gate[0] * (grad_gate[0] - total))
            + chosen[1] * (gate[1] * (grad_gate[1] - total))
        ).astype(BF16)
        hook_two()
        a2a_finish(5 + 2 * l, dr_b.at[l])
        gain_one, gain_two = gains(l)
        returned = dr_b[l].reshape(EXPERTS * SLOTS, D)
        grad_second = nn(p_t[l, 0] + p_t[l, 1], returned) + nt(grad_logits, sh[l, :, 2048:2176])
        normed, inverse = normalize(hid[l])
        second_in = (normed * gain_two).astype(BF16)
        gain_two_grad = jnp.sum(grad_second * normed, axis=0, keepdims=True)
        grad_hidden = grad_out + norm_back(grad_second * gain_two, normed, inverse)
        grad_mixed = grad_hidden.astype(BF16)
        router_grad = tn(second_in, grad_logits)
        grad_heads = nt(grad_mixed, sh[l, :, 1536:2048]).astype(BF16)
        for j in range(4):
            gs[l, j, 128:256, 384:896] = tn(
                o_s[l, :, j * 128:(j + 1) * 128], grad_mixed
            ).astype(BF16)
        for pair in range(4):
            at = pair * 128
            q = qkv_s[l, :, at:at + 128]
            k = qkv_s[l, :, 512 + at:640 + at]
            v = qkv_s[l, :, 1024 + at:1152 + at]
            do = grad_heads[:, at:at + 128]
            grads = []
            for half in range(2):
                scores = nt(k, q * halves[half]) * (HEAD_DIM ** -0.5) + bias[...]
                raised = jnp.exp(scores - jnp.max(scores, axis=0, keepdims=True))
                chance = raised / jnp.sum(raised, axis=0, keepdims=True)
                grad_value = nn(chance.astype(BF16), do)
                grad_chance = nt(v, do * halves[half])
                cross = jnp.sum(chance * grad_chance, axis=0, keepdims=True)
                grad_scores = (chance * (grad_chance - cross)).astype(BF16)
                grad_key = nn(grad_scores, q) * (HEAD_DIM ** -0.5)
                grad_query = tn(grad_scores, k) * (HEAD_DIM ** -0.5)
                grads.append((grad_query, grad_key, grad_value))
            for part in range(3):
                both = jnp.where(first_half, grads[0][part], grads[1][part])
                dqkv[:, part * 512 + at:part * 512 + at + 128] = both.astype(BF16)
        rows_in = (x[...] if l == 0 else lo[0]).astype(F32)
        normed, inverse = normalize(rows_in)
        first_in = (normed * gain_one).astype(BF16)
        grad_first = nt(dqkv[...], sh[l, :, 0:1536])
        gain_one_grad = jnp.sum(grad_first * normed, axis=0, keepdims=True)
        grad_in = grad_hidden + norm_back(grad_first * gain_one, normed, inverse)
        li[l] = grad_in.astype(BF16)
        row8 = iota((8, D), 0)
        both = jnp.where(row8 == 0.0, gain_one_grad, jnp.where(row8 == 1.0, gain_two_grad, 0.0))
        narrow = (router_grad + tn(both.astype(BF16), select)).astype(BF16)
        for j in range(4):
            part = tn(first_in[:, j * 128:(j + 1) * 128], dqkv[...]).astype(BF16)
            gs[l, j, 0:128, :] = part[:, 0:WIDE]
            gs[l, j, 128:256, 0:384] = part[:, WIDE:1536]
            gs[l, j, 128:256, 896:1024] = narrow[j * 128:(j + 1) * 128]
            gs[l, j, 128:256, 1024:1152] = jnp.zeros((128, 128), BF16)
        gs_a(l)

    def exchange(mine, out, send, recv):
        local(mine.at[s], out.at[s], recv)
        put(mine.at[1 - s], out.at[s], send, recv, other)

    def nothing():
        return None

    forward(0)
    weights_start(1)
    forward(1)
    exchange(lo, lout, LO_S, LO_R)
    backward(1, cot[...].astype(F32), nothing, nothing)

    def first_hook():
        gw_b(1)
        gs_b(1)

    def second_hook():
        gs_c(1)

    def before_layer_zero():
        first_hook()
        gw_sent(1)

    backward(0, li[1].astype(F32), before_layer_zero, second_hook)
    exchange(li, lig, LI_S, LI_R)
    gw_b(0)
    gs_b(0)
    gs_c(0)
    gs_d()
    gw_sent(0)
    gs_sent(1)
    gs_sent(0)
    wait(sh.at[0, pl.ds(0, 384)], SH_S)
    wait(w.at[0, pl.ds(0, 3)], W_S)
    wait(gd.at[pl.ds(0, 15)], GSD_S)
    wait(gd, GSD_R)
    for out, send, recv in ((lout, LO_S, LO_R), (lig, LI_S, LI_R)):
        wait(out, recv)
        wait(out.at[0], send)
    wait(ebuf.at[pl.ds(0, 3)], GWB_R)


def shards(
    images, cotangent, ln1_gain, qkv_weight, out_weight, ln2_gain, router_weight,
    up_weight, down_weight, routes,
):
    section = lax.axis_index("section")
    pad = ((0, T - ROWS), (0, 0))
    x = jnp.pad(lax.dynamic_index_in_dim(images, section, 0, False).reshape(ROWS, D), pad)
    cot = jnp.pad(lax.dynamic_index_in_dim(cotangent, section, 0, False).reshape(ROWS, D), pad)
    rt = jnp.swapaxes(routes[0].reshape(2, ROWS, TOPK), 1, 2).astype(F32)
    rt = jnp.pad(rt, ((0, 0), (0, 6), (0, T - ROWS)), constant_values=-1.0)
    shp = jnp.concatenate(
        [qkv_weight[0], out_weight[0], router_weight[0], ln1_gain[0][:, None],
         ln2_gain[0][:, None], jnp.zeros((128, 94), BF16)], axis=1,
    )
    vmem, anywhere = pl.BlockSpec(memory_space=pltpu.VMEM), pl.BlockSpec(memory_space=pl.ANY)
    slots = (2, EXPERTS, SLOTS, D)
    scratch = [
        pltpu.VMEM((2, 4, 2, 512, D), BF16),
        pltpu.VMEM((2, D, SHARED), BF16),
        pltpu.VMEM((2, 8, T), F32), pltpu.VMEM((2, T, 128), F32),
        pltpu.VMEM((T, T), F32),
        pltpu.VMEM((2, 2, EXPERTS * SLOTS, T), BF16), pltpu.VMEM((2, 2, T, EXPERTS * SLOTS), BF16),
        pltpu.VMEM((2, T, 3 * D), BF16), pltpu.VMEM((2, T, D), BF16),
        pltpu.VMEM((2, T, D), F32), pltpu.VMEM((2, 2, T, D), BF16),
        pltpu.VMEM((2, T, 128), F32),
        pltpu.VMEM(slots, BF16), pltpu.VMEM(slots, BF16),
        pltpu.VMEM(slots, BF16), pltpu.VMEM(slots, BF16),
        pltpu.VMEM(slots[1:], BF16), pltpu.VMEM((EXPERTS * SLOTS, D), F32),
        pltpu.VMEM((4, 512, 512), BF16), pltpu.VMEM((4, 512, 512), F32),
        pltpu.VMEM((4, 512, 512), BF16), pltpu.VMEM((T, 3 * D), BF16),
        pltpu.VMEM((4, 2, 512, D), BF16), pltpu.VMEM((2, 2, 2, 512, D), BF16),
        pltpu.VMEM((2, 4, 256, WIDE), BF16), pltpu.VMEM((2, 2, 256, WIDE), BF16),
        pltpu.VMEM((2, 16, 2, 16, WIDE), BF16),
        pltpu.VMEM((2, 2, 16, WIDE), BF16), pltpu.VMEM((4, 16, WIDE), BF16),
        pltpu.VMEM((16, WIDE), BF16),
        pltpu.VMEM((2, T, D), BF16), pltpu.VMEM((2, T, D), BF16),
        pltpu.SemaphoreType.DMA((SEMS,)),
    ]
    lout, lig, ebuf, gd = pl.pallas_call(
        kernel,
        out_shape=(
            jax.ShapeDtypeStruct((2, T, D), BF16),
            jax.ShapeDtypeStruct((2, T, D), BF16),
            jax.ShapeDtypeStruct((4, 2, 512, D), BF16),
            jax.ShapeDtypeStruct((16, 16, WIDE), BF16),
        ),
        in_specs=[vmem, vmem, vmem, anywhere, anywhere, anywhere],
        out_specs=(anywhere,) * 4,
        scratch_shapes=scratch,
        compiler_params=pltpu.CompilerParams(
            has_side_effects=True, vmem_limit_bytes=63 * 1024 * 1024
        ),
    )(x, cot, rt, shp, up_weight[0], down_weight[0])
    shape_out = (1, 2) + images.shape[1:]
    layer_out = lout[:, :ROWS].reshape(shape_out)
    layer_in_grad = lig[:, :ROWS].reshape(shape_out)
    wide = ebuf.astype(F32)
    sums = (wide[0::2] + wide[1::2])
    gathered = gd.reshape(256, WIDE)
    flat = jnp.concatenate([gathered[:128], gathered[128:]], axis=1).astype(F32)
    return (
        layer_out,
        layer_in_grad,
        flat[:, 2080][None],
        flat[:, 0:1536][None],
        flat[:, 1536:2048][None],
        flat[:, 2081][None],
        flat[:, 2048:2080][None],
        sums[:, 0][None],
        sums[:, 1][None],
    )


def solution(mesh):
    in_specs = (
        P(None, ("expert", "shard"), None, None),
        P(None, ("expert", "shard"), None, None),
        P("section", "shard"),
        P("section", "shard", None),
        P("section", "shard", None),
        P("section", "shard"),
        P("section", "shard", None),
        P("section", "expert", "shard", None),
        P("section", "expert", "shard", None),
        P("section", None, ("expert", "shard"), None, None),
    )
    out_specs = (
        P("section", None, ("expert", "shard"), None, None),
        P("section", None, ("expert", "shard"), None, None),
        P("section", "shard"),
        P("section", "shard", None),
        P("section", "shard", None),
        P("section", "shard"),
        P("section", "shard", None),
        P("section", "expert", "shard", None),
        P("section", "expert", "shard", None),
    )
    return jax.shard_map(shards, mesh=mesh, in_specs=in_specs, out_specs=out_specs, check_vma=False)
```

```python
import jax
import jax.numpy as jnp
from jax import lax
from jax.experimental import pallas as pl
from jax.experimental.pallas import tpu as pltpu
from jax.sharding import PartitionSpec as P

HEADS = 8
HEAD_DIM = 64
TOPK = 2
SEQ = 50
ROWS = 200
T = 256
D = 512
EXPERTS = 32
SLOTS = 16
SHARED = 2176
WIDE = 1152
EPS = 1e-06
F32 = jnp.float32
BF16 = jnp.bfloat16
MESH = pl.DeviceIdType.MESH


def nn(a, b):
    return lax.dot_general(a, b, (((1,), (0,)), ((), ())), preferred_element_type=F32)


def nt(a, b):
    return lax.dot_general(a, b, (((1,), (1,)), ((), ())), preferred_element_type=F32)


def tn(a, b):
    return lax.dot_general(a, b, (((0,), (0,)), ((), ())), preferred_element_type=F32)


def iota(shape, dim):
    return lax.broadcasted_iota(jnp.int32, shape, dim).astype(F32)


def one(condition):
    return jnp.where(condition, 1.0, 0.0)


def normalize(values):
    shifted = values - jnp.mean(values, axis=-1, keepdims=True)
    inverse = lax.rsqrt(jnp.mean(shifted * shifted, axis=-1, keepdims=True) + EPS)
    return shifted * inverse, inverse


def norm_back(grad, normed, inverse):
    mean_grad = jnp.mean(grad, axis=-1, keepdims=True)
    mean_cross = jnp.mean(grad * normed, axis=-1, keepdims=True)
    return inverse * (grad - mean_grad - normed * mean_cross)


ROOT = 0.7978845608028654
CUBE = 0.044715


def gelu(x):
    return 0.5 * x * (1.0 + jnp.tanh(ROOT * (x + CUBE * x * x * x)))


def gelu_both(x):
    square = x * x
    bent = jnp.tanh(ROOT * x * (1.0 + CUBE * square))
    half = 0.5 * (1.0 + bent)
    slope = half + 0.5 * x * (1.0 - bent * bent) * (ROOT * (1.0 + 3.0 * CUBE * square))
    return x * half, slope


A2A_S, A2A_R = 0, 8
ROUTE_S, ROUTE_R = 16, 17
SH_S, SH_R, SHF_S, SHF_R = 18, 19, 21, 23
W_S, W_R, WF_S, WF_R = 25, 26, 28, 30
GWA_S, GWA_R, GWB_S, GWB_R = 32, 36, 40, 44
GSA_S, GSA_R, GSB_S, GSB_R = 46, 48, 50, 52
GSC_S, GSC_R, GSD_S, GSD_R = 54, 58, 59, 60
LO_S, LO_R, LI_S, LI_R = 61, 62, 63, 64
SHX_S, SHX_R = 65, 67
SEMS = 69


def kernel(
    x, cot, rt, shp, up, dn,
    lout, lig, eb_up0, eb_up1, eb_dn0, eb_dn1, gd,
    w, sh, rts, rcol, bias, d_t, p_t,
    qkv_s, o_s, hid, pick, gat,
    rows_b, ret_b, g_b, dr_b, sbuf, acc,
    act_t, gp_t, dp_t, dqkv,
    gw, gwa, gs, gsa, gsb, gsc_s, gsc, gd_s, lo, li, sem,
):
    s, e, h = lax.axis_index("section"), lax.axis_index("expert"), lax.axis_index("shard")
    zh, c = lax.div(h, 2), lax.rem(h, 2)
    me = e * 2 + s
    sibling = (s, e, 2 * zh + 1 - c)
    other = (1 - s, e, h)

    def put(src, dst, send, recv, device):
        pltpu.make_async_remote_copy(
            src_ref=src, dst_ref=dst, send_sem=sem.at[send], recv_sem=sem.at[recv],
            device_id=device, device_id_type=MESH,
        ).start()

    def local(src, dst, recv):
        pltpu.make_async_copy(src, dst, sem.at[recv]).start()

    def wait(ref, number):
        pltpu.make_async_copy(ref, ref, sem.at[number]).wait()

    def put_or_local(own, src, dst, send, recv, device, here=None):
        @pl.when(own)
        def _():
            local(src, dst, recv if here is None else here)

        @pl.when(jnp.logical_not(own))
        def _():
            put(src, dst, send, recv, device)

    def wait_unless(own, ref, number):
        @pl.when(jnp.logical_not(own))
        def _():
            wait(ref, number)

    def a2a_start(phase, dst):
        local(sbuf.at[me], dst.at[me], A2A_R + phase)

        def step(i, carry):
            t = lax.rem(me + i, EXPERTS)
            put(sbuf.at[t], dst.at[me], A2A_S + phase, A2A_R + phase,
                (lax.rem(t, 2), lax.div(t, 2), h))
            return carry

        lax.fori_loop(1, EXPERTS, step, 0)

    def a2a_finish(phase, dst):
        wait(dst, A2A_R + phase)
        wait(sbuf.at[pl.ds(0, EXPERTS - 1)], A2A_S + phase)

    barrier = pltpu.get_barrier_semaphore()

    def greet(i, carry):
        t = lax.rem(me + i, EXPERTS)
        pl.semaphore_signal(
            barrier, inc=1, device_id=(lax.rem(t, 2), lax.div(t, 2), h), device_id_type=MESH
        )
        return carry

    lax.fori_loop(1, EXPERTS, greet, 0)
    for to_s in range(2):
        for i in range(1, 4):
            pl.semaphore_signal(
                barrier, inc=1, device_id=(to_s, e, lax.rem(h + i, 4)), device_id_type=MESH
            )

    def image_of(index):
        return one(index >= 50) + one(index >= 100) + one(index >= 150) + one(index >= 200)

    bias[...] = jnp.where(
        image_of(iota((T, T), 0)) == image_of(iota((T, T), 1)), 0.0, -1e30
    )
    lane = iota((T, 128), 1)
    first_half = lane < 64.0
    half_row = iota((1, 128), 1)
    halves = (one(half_row < 64.0).astype(BF16), one(half_row >= 64.0).astype(BF16))
    sel_row, sel_lane = iota((8, 128), 0), iota((8, 128), 1)
    select = one(sel_lane == sel_row + 32.0) * one(sel_row < 2.0)
    select = select.astype(BF16)
    rts[s] = rt[s]
    pl.semaphore_wait(barrier, EXPERTS - 1 + 6)

    put(rt.at[1 - s], rts.at[s], ROUTE_S, ROUTE_R, other)
    own_rows = pl.ds(pl.multiple_of(h * 128, 128), 128)
    own_columns = pl.ds(pl.multiple_of(e * 128, 128), 128)
    for layer in range(2):
        @pl.when(s == layer)
        def _():
            for to_s in range(2):
                for to_zh in range(2):
                    for columns in (own_columns, pl.ds(2048, 128)):
                        put_or_local(
                            jnp.logical_and(s == to_s, zh == to_zh),
                            shp.at[:, columns], sh.at[layer, own_rows, columns],
                            SH_S, SH_R + layer, (to_s, e, 2 * to_zh + c),
                        )

    def weights_start(layer, sections):
        @pl.when(s == layer)
        def _():
            for to_s in sections:
                for to_zh in range(2):
                    own = jnp.logical_and(s == to_s, zh == to_zh)
                    device = (to_s, e, 2 * to_zh + c)
                    put_or_local(own, up.at[to_s], w.at[layer, h, 0], W_S, W_R + layer, device)
                    put_or_local(own, dn.at[to_s], w.at[layer, h, 1], W_S, W_R + layer, device)

    weights_start(0, (0, 1))
    weights_start(1, (0,))

    def peers(step):
        def body(i, carry):
            step(lax.rem(e + i, 16))
            return carry

        lax.fori_loop(1, 16, body, 0)

    def shared_part(l, from_zh, columns):
        rows = pl.ds(pl.multiple_of((2 * from_zh + c) * 128, 128), 128)
        return sh.at[l, rows, columns]

    def shared_across(l):
        wait(sh.at[l, pl.ds(0, 256), pl.ds(0, 256)], SH_R + l)

        def step(to_e):
            for from_zh in range(2):
                part = shared_part(l, from_zh, own_columns)
                put(part, part, SHX_S + l, SHX_R + l, (s, to_e, h))

        peers(step)

    def shared_forward(l):
        across = sh.at[l, pl.ds(0, 256), pl.ds(0, 1920)]
        wait(across, SHX_R + l)
        for from_zh in range(2):
            part = shared_part(l, from_zh, pl.ds(0, SHARED))
            put(part, part, SHF_S + l, SHF_R + l, sibling)
        wait(sh.at[l, pl.ds(0, 256)], SHF_R + l)
        wait(sh.at[l, pl.ds(0, 256)], SHF_S + l)
        wait(across, SHX_S + l)

    shared_across(0)
    wait(rts.at[0], ROUTE_R)
    wait(rts.at[0], ROUTE_S)
    upper = one(iota((T, T), 0) < iota((T, T), 1)).astype(BF16)
    eye = one(sel_lane == sel_row).astype(BF16)
    for l in range(2):
        route = rts[l]
        number = iota((EXPERTS, T), 0)
        chosen = [one(route[k:k + 1] == number) for k in range(2)]
        earlier = nn((chosen[0] + chosen[1]).astype(BF16), upper)
        slot = [jnp.sum(earlier * chosen[k], axis=0, keepdims=True) for k in range(2)]
        slot_number = iota((EXPERTS * SLOTS, T), 0)
        for k in range(2):
            d_t[l, k] = one(slot_number == route[k:k + 1] * SLOTS + slot[k]).astype(BF16)
        row8 = iota((8, T), 0)
        listing = jnp.where(
            row8 == 0.0, route[0:1],
            jnp.where(row8 == 1.0, route[1:2],
                      jnp.where(row8 == 2.0, slot[0], jnp.where(row8 == 3.0, slot[1], 0.0))),
        )
        columns = tn(listing.astype(BF16), eye)
        rcol[l] = columns
        lane_number = iota((T, EXPERTS * SLOTS), 1)
        for k in range(2):
            target = columns[:, k:k + 1] * SLOTS + columns[:, 2 + k:3 + k]
            p_t[l, k] = one(lane_number == target).astype(BF16)

    def choices(l):
        columns = rcol[l]
        return [one(lane == columns[:, k:k + 1]) for k in range(2)]

    def gains(l):
        rows = nt(select, sh[l, :, 2048:2176])
        return rows[0:1], rows[1:2]

    def weights_forward(l):
        wait(w.at[l, pl.ds(0, 2)], W_R + l)
        for from_zh in range(2):
            part = w.at[l, 2 * from_zh + c]
            put(part, part, WF_S + l, WF_R + l, sibling)

    def weights_finish(l):
        for number in (WF_R + l, WF_S + l):
            wait(w.at[l, pl.ds(0, 2)], number)

    def forward(l):
        rows_in = (x[...] if l == 0 else lo[0]).astype(F32)
        normed, _ = normalize(rows_in)
        shared_forward(l)
        if l == 0:
            shared_across(1)
        gain_one, gain_two = gains(l)
        first_in = (normed * gain_one).astype(BF16)
        qkv_s[l] = nn(first_in, sh[l, :, 0:1536]).astype(BF16)
        for pair in range(4):
            at = pair * 128
            q = qkv_s[l, :, at:at + 128]
            k = qkv_s[l, :, 512 + at:640 + at]
            v = qkv_s[l, :, 1024 + at:1152 + at]
            outs = []
            for half in range(2):
                scores = nt(q * halves[half], k) * (HEAD_DIM ** -0.5) + bias[...]
                raised = jnp.exp(scores - jnp.max(scores, axis=-1, keepdims=True))
                chance = raised / jnp.sum(raised, axis=-1, keepdims=True)
                outs.append(nn(chance.astype(BF16), v))
            o_s[l, :, at:at + 128] = jnp.where(first_half, outs[0], outs[1]).astype(BF16)
        hidden = rows_in + nn(o_s[l], sh[l, :, 1536:2048])
        hid[l] = hidden
        normed, _ = normalize(hidden)
        second_in = (normed * gain_two).astype(BF16)
        sbuf[...] = nn(d_t[l, 0] + d_t[l, 1], second_in).astype(BF16).reshape(EXPERTS, SLOTS, D)
        a2a_start(2 * l, rows_b.at[l])
        logits = nn(second_in, sh[l, :, 2048:2176])
        picked = [jnp.sum(ch * logits, axis=1, keepdims=True) for ch in choices(l)]
        top = jnp.maximum(picked[0], picked[1])
        raised = [jnp.exp(value - top) for value in picked]
        total = raised[0] + raised[1]
        gate = [value / total for value in raised]
        gat[l] = jnp.where(lane == 0.0, gate[0], jnp.where(lane == 1.0, gate[1], 0.0))
        weights_forward(l)
        a2a_finish(2 * l, rows_b.at[l])
        weights_finish(l)
        if l == 0:
            weights_start(1, (1,))
        acc[...] = jnp.zeros_like(acc)

        def piece(j, carry):
            before = nt(rows_b[l].reshape(EXPERTS * SLOTS, D), w[l, j, 0])
            acc[...] += nn(gelu(before).astype(BF16), w[l, j, 1])
            return carry

        lax.fori_loop(0, 4, piece, 0)
        sbuf[...] = acc[...].astype(BF16).reshape(EXPERTS, SLOTS, D)
        a2a_start(2 * l + 1, ret_b.at[l])
        a2a_finish(2 * l + 1, ret_b.at[l])
        returned = ret_b[l].reshape(EXPERTS * SLOTS, D)
        result = hid[l]
        for k in range(2):
            mine = nn(p_t[l, k], returned)
            pick[l, k] = mine.astype(BF16)
            result = result + gat[l, :, k:k + 1] * mine
        lo[l] = result.astype(BF16)

    def gw_a(l, to_zh):
        number = 2 * l + to_zh
        put(gw.at[2 * to_zh + 1 - c], gwa.at[l, to_zh], GWA_S + number, GWA_R + number, sibling)

    def gw_b(l):
        for to_zh in range(2):
            j = 2 * to_zh + c
            number = 2 * l + to_zh
            own = jnp.logical_and(s == l, zh == to_zh)
            wait(gwa.at[l, to_zh], GWA_R + number)
            gw[j] = (gw[j].astype(F32) + gwa[l, to_zh].astype(F32)).astype(BF16)
            send = GWB_S + number
            for from_zh, outs in enumerate(((eb_up0, eb_dn0), (eb_up1, eb_dn1))):
                @pl.when(zh == from_zh)
                def _():
                    for u in range(2):
                        put_or_local(own, gw.at[j, u], outs[u].at[s], send, GWB_R, (l, e, j), send)

    def gw_sent(l):
        for to_zh in range(2):
            wait(gwa.at[l, to_zh], GWA_S + 2 * l + to_zh)
            wait(gw.at[0], GWB_S + 2 * l + to_zh)

    def gs_a(l):
        for to_zh in range(2):
            put(gs.at[l, 2 * to_zh + 1 - c], gsa.at[l, to_zh], GSA_S + l, GSA_R + l, sibling)

    def gs_b(l):
        wait(gsa.at[l], GSA_R + l)
        for to_zh in range(2):
            j = 2 * to_zh + c
            gs[l, j] = (gs[l, j].astype(F32) + gsa[l, to_zh].astype(F32)).astype(BF16)

        def part(to_zh, to_e):
            return gs.at[l, 2 * to_zh + c, pl.ds(pl.multiple_of(to_e * 16, 16), 16)]

        def step(to_e):
            for to_zh in range(2):
                put(part(to_zh, to_e), gsb.at[l, e, to_zh], GSB_S + l, GSB_R + l, (s, to_e, h))

        for to_zh in range(2):
            local(part(to_zh, e), gsb.at[l, e, to_zh], GSB_R + l)
        peers(step)

    def gs_c(l):
        wait(gsb.at[l], GSB_R + l)
        total = gsb[l, 0].astype(F32)
        for source in range(1, 16):
            total = total + gsb[l, source].astype(F32)
        gsc_s[l] = total.astype(BF16)
        for to_zh in range(2):
            own = jnp.logical_and(s == l, zh == to_zh)
            put_or_local(own, gsc_s.at[l, to_zh], gsc.at[2 * s + zh], GSC_S + 2 * l + to_zh, GSC_R,
                         (l, e, 2 * to_zh + c))

    def gs_d():
        wait(gsc, GSC_R)
        total = gsc[0].astype(F32)
        for source in range(1, 4):
            total = total + gsc[source].astype(F32)
        gd_s[...] = total.astype(BF16)
        local(gd_s, gd.at[e], GSD_R)
        peers(lambda to_e: put(gd_s, gd.at[e], GSD_S, GSD_R, (s, to_e, h)))

    def gs_sent(l):
        wait(gsa.at[l], GSA_S + l)
        wait(gsb.at[l, pl.ds(0, 15)], GSB_S + l)
        for to_zh in range(2):
            wait_unless(jnp.logical_and(s == l, zh == to_zh), gsc_s.at[l, to_zh], GSC_S + 2 * l + to_zh)

    def backward(l, grad_out, hook_one, hook_two):
        gate = [gat[l, :, k:k + 1] for k in range(2)]
        grad_gate = [
            jnp.sum(grad_out * pick[l, k].astype(F32), axis=-1, keepdims=True) for k in range(2)
        ]
        copies = [(gate[k] * grad_out).astype(BF16) for k in range(2)]
        sent = nn(d_t[l, 0], copies[0]) + nn(d_t[l, 1], copies[1])
        sbuf[...] = sent.astype(BF16).reshape(EXPERTS, SLOTS, D)
        a2a_start(4 + 2 * l, g_b.at[l])

        def again(j, carry):
            before = nt(w[l, j, 0], rows_b[l].reshape(EXPERTS * SLOTS, D))
            active, slope = gelu_both(before)
            act_t[j] = active.astype(BF16)
            gp_t[j] = slope
            return carry

        lax.fori_loop(0, 4, again, 0)
        hook_one()
        a2a_finish(4 + 2 * l, g_b.at[l])
        acc[...] = jnp.zeros_like(acc)

        def back(j, carry):
            grad_active = nt(w[l, j, 1], g_b[l].reshape(EXPERTS * SLOTS, D))
            grad_before = (grad_active * gp_t[j]).astype(BF16)
            dp_t[j] = grad_before
            acc[...] += tn(grad_before, w[l, j, 0])
            return carry

        lax.fori_loop(0, 4, back, 0)
        sbuf[...] = acc[...].astype(BF16).reshape(EXPERTS, SLOTS, D)
        a2a_start(5 + 2 * l, dr_b.at[l])

        def weight_grads(i, carry):
            j = 2 * lax.rem(i, 2) + jnp.where(i < 2, 1 - c, c)
            gw[j, 1] = nn(act_t[j], g_b[l].reshape(EXPERTS * SLOTS, D)).astype(BF16)
            gw[j, 0] = nn(dp_t[j], rows_b[l].reshape(EXPERTS * SLOTS, D)).astype(BF16)
            for to_zh in range(2):
                @pl.when(i == to_zh)
                def _():
                    gw_a(l, to_zh)
            return carry

        if l == 0:
            gw_sent(1)
        lax.fori_loop(0, 4, weight_grads, 0)
        total = gate[0] * grad_gate[0] + gate[1] * grad_gate[1]
        chosen = choices(l)
        grad_logits = (
            chosen[0] * (gate[0] * (grad_gate[0] - total))
            + chosen[1] * (gate[1] * (grad_gate[1] - total))
        ).astype(BF16)
        gw_b(l)
        hook_two()
        a2a_finish(5 + 2 * l, dr_b.at[l])
        gain_one, gain_two = gains(l)
        returned = dr_b[l].reshape(EXPERTS * SLOTS, D)
        grad_second = nn(p_t[l, 0] + p_t[l, 1], returned) + nt(grad_logits, sh[l, :, 2048:2176])
        normed, inverse = normalize(hid[l])
        second_in = (normed * gain_two).astype(BF16)
        gain_two_grad = jnp.sum(grad_second * normed, axis=0, keepdims=True)
        grad_hidden = grad_out + norm_back(grad_second * gain_two, normed, inverse)
        grad_mixed = grad_hidden.astype(BF16)
        router_grad = tn(second_in, grad_logits)
        grad_heads = nt(grad_mixed, sh[l, :, 1536:2048]).astype(BF16)
        for j in range(4):
            gs[l, j, 128:256, 384:896] = tn(
                o_s[l, :, j * 128:(j + 1) * 128], grad_mixed
            ).astype(BF16)
        for pair in range(4):
            at = pair * 128
            q = qkv_s[l, :, at:at + 128]
            k = qkv_s[l, :, 512 + at:640 + at]
            v = qkv_s[l, :, 1024 + at:1152 + at]
            do = grad_heads[:, at:at + 128]
            grads = []
            for half in range(2):
                scores = nt(k, q * halves[half]) * (HEAD_DIM ** -0.5) + bias[...]
                raised = jnp.exp(scores - jnp.max(scores, axis=0, keepdims=True))
                chance = raised / jnp.sum(raised, axis=0, keepdims=True)
                grad_value = nn(chance.astype(BF16), do)
                grad_chance = nt(v, do * halves[half])
                cross = jnp.sum(chance * grad_chance, axis=0, keepdims=True)
                grad_scores = (chance * (grad_chance - cross)).astype(BF16)
                grad_key = nn(grad_scores, q) * (HEAD_DIM ** -0.5)
                grad_query = tn(grad_scores, k) * (HEAD_DIM ** -0.5)
                grads.append((grad_query, grad_key, grad_value))
            for part in range(3):
                both = jnp.where(first_half, grads[0][part], grads[1][part])
                dqkv[:, part * 512 + at:part * 512 + at + 128] = both.astype(BF16)
        rows_in = (x[...] if l == 0 else lo[0]).astype(F32)
        normed, inverse = normalize(rows_in)
        first_in = (normed * gain_one).astype(BF16)
        grad_first = nt(dqkv[...], sh[l, :, 0:1536])
        gain_one_grad = jnp.sum(grad_first * normed, axis=0, keepdims=True)
        grad_in = grad_hidden + norm_back(grad_first * gain_one, normed, inverse)
        li[l] = grad_in.astype(BF16)
        row8 = iota((8, D), 0)
        both = jnp.where(row8 == 0.0, gain_one_grad, jnp.where(row8 == 1.0, gain_two_grad, 0.0))
        narrow = (router_grad + tn(both.astype(BF16), select)).astype(BF16)
        for j in range(4):
            part = tn(first_in[:, j * 128:(j + 1) * 128], dqkv[...]).astype(BF16)
            gs[l, j, 0:128, :] = part[:, 0:WIDE]
            gs[l, j, 128:256, 0:384] = part[:, WIDE:1536]
            gs[l, j, 128:256, 896:1024] = narrow[j * 128:(j + 1) * 128]
            gs[l, j, 128:256, 1024:1152] = jnp.zeros((128, 128), BF16)
        gs_a(l)

    def exchange(mine, out, send, recv):
        local(mine.at[s], out.at[s], recv)
        put(mine.at[1 - s], out.at[s], send, recv, other)

    def nothing():
        return None

    forward(0)
    forward(1)
    exchange(lo, lout, LO_S, LO_R)
    backward(1, cot[...].astype(F32), nothing, nothing)

    def first_hook():
        gs_b(1)

    def second_hook():
        gs_c(1)

    backward(0, li[1].astype(F32), first_hook, second_hook)
    exchange(li, lig, LI_S, LI_R)
    gs_b(0)
    gs_c(0)
    gs_d()
    gw_sent(0)
    gs_sent(1)
    gs_sent(0)
    wait(sh.at[0, pl.ds(0, 384), pl.ds(0, 256)], SH_S)
    wait(w.at[0, pl.ds(0, 3)], W_S)
    wait(gd.at[pl.ds(0, 15)], GSD_S)
    wait(gd, GSD_R)
    for out, send, recv in ((lout, LO_S, LO_R), (lig, LI_S, LI_R)):
        wait(out, recv)
        wait(out.at[0], send)
    wait(gw.at[pl.ds(0, 3)], GWB_R)


def shards(
    images, cotangent, ln1_gain, qkv_weight, out_weight, ln2_gain, router_weight,
    up_weight, down_weight, routes,
):
    section = lax.axis_index("section")
    pad = ((0, T - ROWS), (0, 0))
    x = jnp.pad(lax.dynamic_index_in_dim(images, section, 0, False).reshape(ROWS, D), pad)
    cot = jnp.pad(lax.dynamic_index_in_dim(cotangent, section, 0, False).reshape(ROWS, D), pad)
    rt = jnp.swapaxes(routes[0].reshape(2, ROWS, TOPK), 1, 2).astype(F32)
    rt = jnp.pad(rt, ((0, 0), (0, 6), (0, T - ROWS)), constant_values=-1.0)
    shp = jnp.concatenate(
        [qkv_weight[0], out_weight[0], router_weight[0], ln1_gain[0][:, None],
         ln2_gain[0][:, None], jnp.zeros((128, 94), BF16)], axis=1,
    )
    vmem, anywhere = pl.BlockSpec(memory_space=pltpu.VMEM), pl.BlockSpec(memory_space=pl.ANY)
    slots = (2, EXPERTS, SLOTS, D)
    scratch = [
        pltpu.VMEM((2, 4, 2, 512, D), BF16),
        pltpu.VMEM((2, D, SHARED), BF16),
        pltpu.VMEM((2, 8, T), F32), pltpu.VMEM((2, T, 128), F32),
        pltpu.VMEM((T, T), F32),
        pltpu.VMEM((2, 2, EXPERTS * SLOTS, T), BF16), pltpu.VMEM((2, 2, T, EXPERTS * SLOTS), BF16),
        pltpu.VMEM((2, T, 3 * D), BF16), pltpu.VMEM((2, T, D), BF16),
        pltpu.VMEM((2, T, D), F32), pltpu.VMEM((2, 2, T, D), BF16),
        pltpu.VMEM((2, T, 128), F32),
        pltpu.VMEM(slots, BF16), pltpu.VMEM(slots, BF16),
        pltpu.VMEM(slots, BF16), pltpu.VMEM(slots, BF16),
        pltpu.VMEM(slots[1:], BF16), pltpu.VMEM((EXPERTS * SLOTS, D), F32),
        pltpu.VMEM((4, 512, 512), BF16), pltpu.VMEM((4, 512, 512), F32),
        pltpu.VMEM((4, 512, 512), BF16), pltpu.VMEM((T, 3 * D), BF16),
        pltpu.VMEM((4, 2, 512, D), BF16), pltpu.VMEM((2, 2, 2, 512, D), BF16),
        pltpu.VMEM((2, 4, 256, WIDE), BF16), pltpu.VMEM((2, 2, 256, WIDE), BF16),
        pltpu.VMEM((2, 16, 2, 16, WIDE), BF16),
        pltpu.VMEM((2, 2, 16, WIDE), BF16), pltpu.VMEM((4, 16, WIDE), BF16),
        pltpu.VMEM((16, WIDE), BF16),
        pltpu.VMEM((2, T, D), BF16), pltpu.VMEM((2, T, D), BF16),
        pltpu.SemaphoreType.DMA((SEMS,)),
    ]
    lout, lig, up0, up1, dn0, dn1, gd = pl.pallas_call(
        kernel,
        out_shape=(
            jax.ShapeDtypeStruct((2, T, D), BF16),
            jax.ShapeDtypeStruct((2, T, D), BF16),
            jax.ShapeDtypeStruct((2, 512, D), BF16),
            jax.ShapeDtypeStruct((2, 512, D), BF16),
            jax.ShapeDtypeStruct((2, 512, D), BF16),
            jax.ShapeDtypeStruct((2, 512, D), BF16),
            jax.ShapeDtypeStruct((16, 16, WIDE), BF16),
        ),
        in_specs=[vmem, vmem, vmem, anywhere, anywhere, anywhere],
        out_specs=(anywhere,) * 7,
        scratch_shapes=scratch,
        compiler_params=pltpu.CompilerParams(
            has_side_effects=True, collective_id=0, vmem_limit_bytes=63 * 1024 * 1024
        ),
    )(x, cot, rt, shp, up_weight[0], down_weight[0])
    shape_out = (1, 2) + images.shape[1:]
    layer_out = lout[:, :ROWS].reshape(shape_out)
    layer_in_grad = lig[:, :ROWS].reshape(shape_out)
    gathered = gd.reshape(256, WIDE)
    flat = jnp.concatenate([gathered[:128], gathered[128:]], axis=1).astype(F32)
    return (
        layer_out,
        layer_in_grad,
        flat[:, 2080][None],
        flat[:, 0:1536][None],
        flat[:, 1536:2048][None],
        flat[:, 2081][None],
        flat[:, 2048:2080][None],
        (up0.astype(F32) + up1.astype(F32))[None],
        (dn0.astype(F32) + dn1.astype(F32))[None],
    )


def solution(mesh):
    in_specs = (
        P(None, ("expert", "shard"), None, None),
        P(None, ("expert", "shard"), None, None),
        P("section", "shard"),
        P("section", "shard", None),
        P("section", "shard", None),
        P("section", "shard"),
        P("section", "shard", None),
        P("section", "expert", "shard", None),
        P("section", "expert", "shard", None),
        P("section", None, ("expert", "shard"), None, None),
    )
    out_specs = (
        P("section", None, ("expert", "shard"), None, None),
        P("section", None, ("expert", "shard"), None, None),
        P("section", "shard"),
        P("section", "shard", None),
        P("section", "shard", None),
        P("section", "shard"),
        P("section", "shard", None),
        P("section", "expert", "shard", None),
        P("section", "expert", "shard", None),
    )
    return jax.shard_map(shards, mesh=mesh, in_specs=in_specs, out_specs=out_specs, check_vma=False)
```

```python
import jax
import jax.numpy as jnp
from jax import lax
from jax.experimental import pallas as pl
from jax.experimental.pallas import tpu as pltpu
from jax.sharding import PartitionSpec as P

HEADS = 8
HEAD_DIM = 64
TOPK = 2
SEQ = 50
ROWS = 200
T = 256
D = 512
EXPERTS = 32
SLOTS = 16
SHARED = 2176
WIDE = 1152
EPS = 1e-06
F32 = jnp.float32
BF16 = jnp.bfloat16
MESH = pl.DeviceIdType.MESH


def nn(a, b):
    return lax.dot_general(a, b, (((1,), (0,)), ((), ())), preferred_element_type=F32)


def nt(a, b):
    return lax.dot_general(a, b, (((1,), (1,)), ((), ())), preferred_element_type=F32)


def tn(a, b):
    return lax.dot_general(a, b, (((0,), (0,)), ((), ())), preferred_element_type=F32)


def iota(shape, dim):
    return lax.broadcasted_iota(jnp.int32, shape, dim).astype(F32)


def one(condition):
    return jnp.where(condition, 1.0, 0.0)


def normalize(values):
    shifted = values - jnp.mean(values, axis=-1, keepdims=True)
    inverse = lax.rsqrt(jnp.mean(shifted * shifted, axis=-1, keepdims=True) + EPS)
    return shifted * inverse, inverse


def norm_back(grad, normed, inverse):
    mean_grad = jnp.mean(grad, axis=-1, keepdims=True)
    mean_cross = jnp.mean(grad * normed, axis=-1, keepdims=True)
    return inverse * (grad - mean_grad - normed * mean_cross)


ROOT = 0.7978845608028654
CUBE = 0.044715


def gelu(x):
    return 0.5 * x * (1.0 + jnp.tanh(ROOT * (x + CUBE * x * x * x)))


def gelu_both(x):
    square = x * x
    bent = jnp.tanh(ROOT * x * (1.0 + CUBE * square))
    half = 0.5 * (1.0 + bent)
    slope = half + 0.5 * x * (1.0 - bent * bent) * (ROOT * (1.0 + 3.0 * CUBE * square))
    return x * half, slope


A2A_S, A2A_R = 0, 8
ROUTE_S, ROUTE_R = 16, 17
SH_S, SH_R, SHF_S, SHF_R = 18, 19, 21, 23
W_S, W_R, WF_S, WF_R = 25, 26, 28, 30
GWA_S, GWA_R, GWB_S, GWB_R = 32, 36, 40, 44
GSA_S, GSA_R, GSB_S, GSB_R = 46, 48, 50, 52
GSC_S, GSC_R, GSD_S, GSD_R = 54, 58, 59, 60
LO_S, LO_R, LI_S, LI_R = 61, 62, 63, 64
SHX_S, SHX_R = 65, 67
SEMS = 69


def kernel(
    x, cot, rt, shp, up, dn,
    lout, lig, eb_up0, eb_up1, eb_dn0, eb_dn1, gd,
    w, sh, rts, rcol, bias, d_t, p_t,
    qkv_s, o_s, hid, pick, gat,
    rows_b, ret_b, g_b, dr_b, sbuf, acc,
    act_t, gp_t, dp_t, dqkv,
    gw, gwa, gs, gsa, gsb, gsc_s, gsc, gd_s, lo, li, sem,
):
    s, e, h = lax.axis_index("section"), lax.axis_index("expert"), lax.axis_index("shard")
    zh, c = lax.div(h, 2), lax.rem(h, 2)
    me = e * 2 + s
    sibling = (s, e, 2 * zh + 1 - c)
    other = (1 - s, e, h)

    def put(src, dst, send, recv, device):
        pltpu.make_async_remote_copy(
            src_ref=src, dst_ref=dst, send_sem=sem.at[send], recv_sem=sem.at[recv],
            device_id=device, device_id_type=MESH,
        ).start()

    def local(src, dst, recv):
        pltpu.make_async_copy(src, dst, sem.at[recv]).start()

    def wait(ref, number):
        pltpu.make_async_copy(ref, ref, sem.at[number]).wait()

    def put_or_local(own, src, dst, send, recv, device, here=None):
        @pl.when(own)
        def _():
            local(src, dst, recv if here is None else here)

        @pl.when(jnp.logical_not(own))
        def _():
            put(src, dst, send, recv, device)

    def wait_unless(own, ref, number):
        @pl.when(jnp.logical_not(own))
        def _():
            wait(ref, number)

    def a2a_start(phase, dst):
        local(sbuf.at[me], dst.at[me], A2A_R + phase)

        def step(i, carry):
            t = lax.rem(me + i, EXPERTS)
            put(sbuf.at[t], dst.at[me], A2A_S + phase, A2A_R + phase,
                (lax.rem(t, 2), lax.div(t, 2), h))
            return carry

        lax.fori_loop(1, EXPERTS, step, 0)

    def a2a_finish(phase, dst):
        wait(dst, A2A_R + phase)
        wait(sbuf.at[pl.ds(0, EXPERTS - 1)], A2A_S + phase)

    barrier = pltpu.get_barrier_semaphore()

    def greet(i, carry):
        t = lax.rem(me + i, EXPERTS)
        pl.semaphore_signal(
            barrier, inc=1, device_id=(lax.rem(t, 2), lax.div(t, 2), h), device_id_type=MESH
        )
        return carry

    lax.fori_loop(1, EXPERTS, greet, 0)
    for to_s in range(2):
        for i in range(1, 4):
            pl.semaphore_signal(
                barrier, inc=1, device_id=(to_s, e, lax.rem(h + i, 4)), device_id_type=MESH
            )

    def image_of(index):
        return one(index >= 50) + one(index >= 100) + one(index >= 150) + one(index >= 200)

    bias[...] = jnp.where(
        image_of(iota((T, T), 0)) == image_of(iota((T, T), 1)), 0.0, -1e30
    )
    lane = iota((T, 128), 1)
    first_half = lane < 64.0
    half_row = iota((1, 128), 1)
    halves = (one(half_row < 64.0).astype(BF16), one(half_row >= 64.0).astype(BF16))
    sel_row, sel_lane = iota((8, 128), 0), iota((8, 128), 1)
    select = one(sel_lane == sel_row + 32.0) * one(sel_row < 2.0)
    select = select.astype(BF16)
    rts[s] = rt[s]
    pl.semaphore_wait(barrier, EXPERTS - 1 + 6)

    put(rt.at[1 - s], rts.at[s], ROUTE_S, ROUTE_R, other)
    own_rows = pl.ds(pl.multiple_of(h * 128, 128), 128)
    own_columns = pl.ds(pl.multiple_of(e * 128, 128), 128)
    for layer in range(2):
        @pl.when(s == layer)
        def _():
            for to_s in range(2):
                for to_zh in range(2):
                    for columns in (own_columns, pl.ds(2048, 128)):
                        put_or_local(
                            jnp.logical_and(s == to_s, zh == to_zh),
                            shp.at[:, columns], sh.at[layer, own_rows, columns],
                            SH_S, SH_R + layer, (to_s, e, 2 * to_zh + c),
                        )

    def weights_start(layer, sections):
        @pl.when(s == layer)
        def _():
            for to_s in sections:
                for to_zh in range(2):
                    own = jnp.logical_and(s == to_s, zh == to_zh)
                    device = (to_s, e, 2 * to_zh + c)
                    put_or_local(own, up.at[to_s], w.at[layer, h, 0], W_S, W_R + layer, device)
                    put_or_local(own, dn.at[to_s], w.at[layer, h, 1], W_S, W_R + layer, device)

    weights_start(0, (0, 1))
    weights_start(1, (0, 1))

    def peers(step):
        def body(i, carry):
            step(lax.rem(e + i, 16))
            return carry

        lax.fori_loop(1, 16, body, 0)

    def shared_part(l, from_zh, columns):
        rows = pl.ds(pl.multiple_of((2 * from_zh + c) * 128, 128), 128)
        return sh.at[l, rows, columns]

    def shared_across(l):
        wait(sh.at[l, pl.ds(0, 256), pl.ds(0, 256)], SH_R + l)

        def step(to_e):
            for from_zh in range(2):
                part = shared_part(l, from_zh, own_columns)
                put(part, part, SHX_S + l, SHX_R + l, (s, to_e, h))

        peers(step)

    def shared_forward(l):
        across = sh.at[l, pl.ds(0, 256), pl.ds(0, 1920)]
        wait(across, SHX_R + l)
        for from_zh in range(2):
            part = shared_part(l, from_zh, pl.ds(0, SHARED))
            put(part, part, SHF_S + l, SHF_R + l, sibling)
        wait(sh.at[l, pl.ds(0, 256)], SHF_R + l)
        wait(sh.at[l, pl.ds(0, 256)], SHF_S + l)
        wait(across, SHX_S + l)

    shared_across(0)
    wait(rts.at[0], ROUTE_R)
    wait(rts.at[0], ROUTE_S)
    upper = one(iota((T, T), 0) < iota((T, T), 1)).astype(BF16)
    eye = one(sel_lane == sel_row).astype(BF16)
    for l in range(2):
        route = rts[l]
        number = iota((EXPERTS, T), 0)
        chosen = [one(route[k:k + 1] == number) for k in range(2)]
        earlier = nn((chosen[0] + chosen[1]).astype(BF16), upper)
        slot = [jnp.sum(earlier * chosen[k], axis=0, keepdims=True) for k in range(2)]
        slot_number = iota((EXPERTS * SLOTS, T), 0)
        for k in range(2):
            d_t[l, k] = one(slot_number == route[k:k + 1] * SLOTS + slot[k]).astype(BF16)
        row8 = iota((8, T), 0)
        listing = jnp.where(
            row8 == 0.0, route[0:1],
            jnp.where(row8 == 1.0, route[1:2],
                      jnp.where(row8 == 2.0, slot[0], jnp.where(row8 == 3.0, slot[1], 0.0))),
        )
        columns = tn(listing.astype(BF16), eye)
        rcol[l] = columns
        lane_number = iota((T, EXPERTS * SLOTS), 1)
        for k in range(2):
            target = columns[:, k:k + 1] * SLOTS + columns[:, 2 + k:3 + k]
            p_t[l, k] = one(lane_number == target).astype(BF16)

    def choices(l):
        columns = rcol[l]
        return [one(lane == columns[:, k:k + 1]) for k in range(2)]

    def gains(l):
        rows = nt(select, sh[l, :, 2048:2176])
        return rows[0:1], rows[1:2]

    def weights_forward(l):
        wait(w.at[l, pl.ds(0, 2)], W_R + l)
        for from_zh in range(2):
            part = w.at[l, 2 * from_zh + c]
            put(part, part, WF_S + l, WF_R + l, sibling)

    def weights_finish(l):
        for number in (WF_R + l, WF_S + l):
            wait(w.at[l, pl.ds(0, 2)], number)

    def forward(l):
        rows_in = (x[...] if l == 0 else lo[0]).astype(F32)
        normed, _ = normalize(rows_in)
        shared_forward(l)
        if l == 0:
            shared_across(1)
        gain_one, gain_two = gains(l)
        first_in = (normed * gain_one).astype(BF16)
        qkv_s[l] = nn(first_in, sh[l, :, 0:1536]).astype(BF16)
        for pair in range(4):
            at = pair * 128
            q = qkv_s[l, :, at:at + 128]
            k = qkv_s[l, :, 512 + at:640 + at]
            v = qkv_s[l, :, 1024 + at:1152 + at]
            outs = []
            for half in range(2):
                scores = nt(q * halves[half], k) * (HEAD_DIM ** -0.5) + bias[...]
                raised = jnp.exp(scores - jnp.max(scores, axis=-1, keepdims=True))
                chance = raised / jnp.sum(raised, axis=-1, keepdims=True)
                outs.append(nn(chance.astype(BF16), v))
            o_s[l, :, at:at + 128] = jnp.where(first_half, outs[0], outs[1]).astype(BF16)
        hidden = rows_in + nn(o_s[l], sh[l, :, 1536:2048])
        hid[l] = hidden
        normed, _ = normalize(hidden)
        second_in = (normed * gain_two).astype(BF16)
        sbuf[...] = nn(d_t[l, 0] + d_t[l, 1], second_in).astype(BF16).reshape(EXPERTS, SLOTS, D)
        a2a_start(2 * l, rows_b.at[l])
        logits = nn(second_in, sh[l, :, 2048:2176])
        picked = [jnp.sum(ch * logits, axis=1, keepdims=True) for ch in choices(l)]
        top = jnp.maximum(picked[0], picked[1])
        raised = [jnp.exp(value - top) for value in picked]
        total = raised[0] + raised[1]
        gate = [value / total for value in raised]
        gat[l] = jnp.where(lane == 0.0, gate[0], jnp.where(lane == 1.0, gate[1], 0.0))
        weights_forward(l)
        a2a_finish(2 * l, rows_b.at[l])
        weights_finish(l)
        acc[...] = jnp.zeros_like(acc)

        def piece(j, carry):
            before = nt(rows_b[l].reshape(EXPERTS * SLOTS, D), w[l, j, 0])
            acc[...] += nn(gelu(before).astype(BF16), w[l, j, 1])
            return carry

        lax.fori_loop(0, 4, piece, 0)
        sbuf[...] = acc[...].astype(BF16).reshape(EXPERTS, SLOTS, D)
        a2a_start(2 * l + 1, ret_b.at[l])
        a2a_finish(2 * l + 1, ret_b.at[l])
        returned = ret_b[l].reshape(EXPERTS * SLOTS, D)
        result = hid[l]
        for k in range(2):
            mine = nn(p_t[l, k], returned)
            pick[l, k] = mine.astype(BF16)
            result = result + gat[l, :, k:k + 1] * mine
        lo[l] = result.astype(BF16)

    def gw_a(l, to_zh):
        number = 2 * l + to_zh
        put(gw.at[2 * to_zh + 1 - c], gwa.at[l, to_zh], GWA_S + number, GWA_R + number, sibling)

    def gw_b(l):
        for to_zh in range(2):
            j = 2 * to_zh + c
            number = 2 * l + to_zh
            own = jnp.logical_and(s == l, zh == to_zh)
            wait(gwa.at[l, to_zh], GWA_R + number)
            gw[j] = (gw[j].astype(F32) + gwa[l, to_zh].astype(F32)).astype(BF16)
            send = GWB_S + number
            for from_zh, outs in enumerate(((eb_up0, eb_dn0), (eb_up1, eb_dn1))):
                @pl.when(zh == from_zh)
                def _():
                    for u in range(2):
                        put_or_local(own, gw.at[j, u], outs[u].at[s], send, GWB_R, (l, e, j), send)

    def gw_sent(l):
        for to_zh in range(2):
            wait(gwa.at[l, to_zh], GWA_S + 2 * l + to_zh)
            wait(gw.at[0], GWB_S + 2 * l + to_zh)

    def gs_a(l):
        for to_zh in range(2):
            put(gs.at[l, 2 * to_zh + 1 - c], gsa.at[l, to_zh], GSA_S + l, GSA_R + l, sibling)

    def gs_b(l):
        wait(gsa.at[l], GSA_R + l)
        for to_zh in range(2):
            j = 2 * to_zh + c
            gs[l, j] = (gs[l, j].astype(F32) + gsa[l, to_zh].astype(F32)).astype(BF16)

        def part(to_zh, to_e):
            return gs.at[l, 2 * to_zh + c, pl.ds(pl.multiple_of(to_e * 16, 16), 16)]

        def step(to_e):
            for to_zh in range(2):
                put(part(to_zh, to_e), gsb.at[l, e, to_zh], GSB_S + l, GSB_R + l, (s, to_e, h))

        for to_zh in range(2):
            local(part(to_zh, e), gsb.at[l, e, to_zh], GSB_R + l)
        peers(step)

    def gs_c(l):
        wait(gsb.at[l], GSB_R + l)
        total = gsb[l, 0].astype(F32)
        for source in range(1, 16):
            total = total + gsb[l, source].astype(F32)
        gsc_s[l] = total.astype(BF16)
        for to_zh in range(2):
            own = jnp.logical_and(s == l, zh == to_zh)
            put_or_local(own, gsc_s.at[l, to_zh], gsc.at[2 * s + zh], GSC_S + 2 * l + to_zh, GSC_R,
                         (l, e, 2 * to_zh + c))

    def gs_d():
        wait(gsc, GSC_R)
        total = gsc[0].astype(F32)
        for source in range(1, 4):
            total = total + gsc[source].astype(F32)
        gd_s[...] = total.astype(BF16)
        local(gd_s, gd.at[e], GSD_R)
        peers(lambda to_e: put(gd_s, gd.at[e], GSD_S, GSD_R, (s, to_e, h)))

    def gs_sent(l):
        wait(gsa.at[l], GSA_S + l)
        wait(gsb.at[l, pl.ds(0, 15)], GSB_S + l)
        for to_zh in range(2):
            wait_unless(jnp.logical_and(s == l, zh == to_zh), gsc_s.at[l, to_zh], GSC_S + 2 * l + to_zh)

    def backward(l, grad_out, hook_one, hook_two):
        gate = [gat[l, :, k:k + 1] for k in range(2)]
        grad_gate = [
            jnp.sum(grad_out * pick[l, k].astype(F32), axis=-1, keepdims=True) for k in range(2)
        ]
        copies = [(gate[k] * grad_out).astype(BF16) for k in range(2)]
        sent = nn(d_t[l, 0], copies[0]) + nn(d_t[l, 1], copies[1])
        sbuf[...] = sent.astype(BF16).reshape(EXPERTS, SLOTS, D)
        a2a_start(4 + 2 * l, g_b.at[l])

        def again(j, carry):
            before = nt(w[l, j, 0], rows_b[l].reshape(EXPERTS * SLOTS, D))
            active, slope = gelu_both(before)
            act_t[j] = active.astype(BF16)
            gp_t[j] = slope
            return carry

        lax.fori_loop(0, 4, again, 0)
        hook_one()
        a2a_finish(4 + 2 * l, g_b.at[l])
        acc[...] = jnp.zeros_like(acc)

        def back(j, carry):
            grad_active = nt(w[l, j, 1], g_b[l].reshape(EXPERTS * SLOTS, D))
            grad_before = (grad_active * gp_t[j]).astype(BF16)
            dp_t[j] = grad_before
            acc[...] += tn(grad_before, w[l, j, 0])
            return carry

        lax.fori_loop(0, 4, back, 0)
        sbuf[...] = acc[...].astype(BF16).reshape(EXPERTS, SLOTS, D)
        a2a_start(5 + 2 * l, dr_b.at[l])

        def weight_grads(i, carry):
            j = 2 * lax.rem(i, 2) + jnp.where(i < 2, 1 - c, c)
            gw[j, 1] = nn(act_t[j], g_b[l].reshape(EXPERTS * SLOTS, D)).astype(BF16)
            gw[j, 0] = nn(dp_t[j], rows_b[l].reshape(EXPERTS * SLOTS, D)).astype(BF16)
            for to_zh in range(2):
                @pl.when(i == to_zh)
                def _():
                    gw_a(l, to_zh)
            return carry

        if l == 0:
            gw_sent(1)
        lax.fori_loop(0, 4, weight_grads, 0)
        total = gate[0] * grad_gate[0] + gate[1] * grad_gate[1]
        chosen = choices(l)
        grad_logits = (
            chosen[0] * (gate[0] * (grad_gate[0] - total))
            + chosen[1] * (gate[1] * (grad_gate[1] - total))
        ).astype(BF16)
        gw_b(l)
        hook_two()
        a2a_finish(5 + 2 * l, dr_b.at[l])
        gain_one, gain_two = gains(l)
        returned = dr_b[l].reshape(EXPERTS * SLOTS, D)
        grad_second = nn(p_t[l, 0] + p_t[l, 1], returned) + nt(grad_logits, sh[l, :, 2048:2176])
        normed, inverse = normalize(hid[l])
        second_in = (normed * gain_two).astype(BF16)
        gain_two_grad = jnp.sum(grad_second * normed, axis=0, keepdims=True)
        grad_hidden = grad_out + norm_back(grad_second * gain_two, normed, inverse)
        grad_mixed = grad_hidden.astype(BF16)
        router_grad = tn(second_in, grad_logits)
        grad_heads = nt(grad_mixed, sh[l, :, 1536:2048]).astype(BF16)
        for j in range(4):
            gs[l, j, 128:256, 384:896] = tn(
                o_s[l, :, j * 128:(j + 1) * 128], grad_mixed
            ).astype(BF16)
        for pair in range(4):
            at = pair * 128
            q = qkv_s[l, :, at:at + 128]
            k = qkv_s[l, :, 512 + at:640 + at]
            v = qkv_s[l, :, 1024 + at:1152 + at]
            do = grad_heads[:, at:at + 128]
            grads = []
            for half in range(2):
                scores = nt(k, q * halves[half]) * (HEAD_DIM ** -0.5) + bias[...]
                raised = jnp.exp(scores - jnp.max(scores, axis=0, keepdims=True))
                chance = raised / jnp.sum(raised, axis=0, keepdims=True)
                grad_value = nn(chance.astype(BF16), do)
                grad_chance = nt(v, do * halves[half])
                cross = jnp.sum(chance * grad_chance, axis=0, keepdims=True)
                grad_scores = (chance * (grad_chance - cross)).astype(BF16)
                grad_key = nn(grad_scores, q) * (HEAD_DIM ** -0.5)
                grad_query = tn(grad_scores, k) * (HEAD_DIM ** -0.5)
                grads.append((grad_query, grad_key, grad_value))
            for part in range(3):
                both = jnp.where(first_half, grads[0][part], grads[1][part])
                dqkv[:, part * 512 + at:part * 512 + at + 128] = both.astype(BF16)
        rows_in = (x[...] if l == 0 else lo[0]).astype(F32)
        normed, inverse = normalize(rows_in)
        first_in = (normed * gain_one).astype(BF16)
        grad_first = nt(dqkv[...], sh[l, :, 0:1536])
        gain_one_grad = jnp.sum(grad_first * normed, axis=0, keepdims=True)
        grad_in = grad_hidden + norm_back(grad_first * gain_one, normed, inverse)
        li[l] = grad_in.astype(BF16)
        row8 = iota((8, D), 0)
        both = jnp.where(row8 == 0.0, gain_one_grad, jnp.where(row8 == 1.0, gain_two_grad, 0.0))
        narrow = (router_grad + tn(both.astype(BF16), select)).astype(BF16)
        for j in range(4):
            part = tn(first_in[:, j * 128:(j + 1) * 128], dqkv[...]).astype(BF16)
            gs[l, j, 0:128, :] = part[:, 0:WIDE]
            gs[l, j, 128:256, 0:384] = part[:, WIDE:1536]
            gs[l, j, 128:256, 896:1024] = narrow[j * 128:(j + 1) * 128]
            gs[l, j, 128:256, 1024:1152] = jnp.zeros((128, 128), BF16)
        gs_a(l)

    def exchange(mine, out, send, recv):
        local(mine.at[s], out.at[s], recv)
        put(mine.at[1 - s], out.at[s], send, recv, other)

    def nothing():
        return None

    forward(0)
    forward(1)
    exchange(lo, lout, LO_S, LO_R)
    backward(1, cot[...].astype(F32), nothing, nothing)

    def first_hook():
        gs_b(1)

    def second_hook():
        gs_c(1)

    backward(0, li[1].astype(F32), first_hook, second_hook)
    exchange(li, lig, LI_S, LI_R)
    gs_b(0)
    gs_c(0)
    gs_d()
    gw_sent(0)
    gs_sent(1)
    gs_sent(0)
    wait(sh.at[0, pl.ds(0, 384), pl.ds(0, 256)], SH_S)
    wait(w.at[0, pl.ds(0, 3)], W_S)
    wait(gd.at[pl.ds(0, 15)], GSD_S)
    wait(gd, GSD_R)
    for out, send, recv in ((lout, LO_S, LO_R), (lig, LI_S, LI_R)):
        wait(out, recv)
        wait(out.at[0], send)
    wait(gw.at[pl.ds(0, 3)], GWB_R)


def shards(
    images, cotangent, ln1_gain, qkv_weight, out_weight, ln2_gain, router_weight,
    up_weight, down_weight, routes,
):
    section = lax.axis_index("section")
    pad = ((0, T - ROWS), (0, 0))
    x = jnp.pad(lax.dynamic_index_in_dim(images, section, 0, False).reshape(ROWS, D), pad)
    cot = jnp.pad(lax.dynamic_index_in_dim(cotangent, section, 0, False).reshape(ROWS, D), pad)
    rt = jnp.swapaxes(routes[0].reshape(2, ROWS, TOPK), 1, 2).astype(F32)
    rt = jnp.pad(rt, ((0, 0), (0, 6), (0, T - ROWS)), constant_values=-1.0)
    shp = jnp.concatenate(
        [qkv_weight[0], out_weight[0], router_weight[0], ln1_gain[0][:, None],
         ln2_gain[0][:, None], jnp.zeros((128, 94), BF16)], axis=1,
    )
    vmem, anywhere = pl.BlockSpec(memory_space=pltpu.VMEM), pl.BlockSpec(memory_space=pl.ANY)
    slots = (2, EXPERTS, SLOTS, D)
    scratch = [
        pltpu.VMEM((2, 4, 2, 512, D), BF16),
        pltpu.VMEM((2, D, SHARED), BF16),
        pltpu.VMEM((2, 8, T), F32), pltpu.VMEM((2, T, 128), F32),
        pltpu.VMEM((T, T), F32),
        pltpu.VMEM((2, 2, EXPERTS * SLOTS, T), BF16), pltpu.VMEM((2, 2, T, EXPERTS * SLOTS), BF16),
        pltpu.VMEM((2, T, 3 * D), BF16), pltpu.VMEM((2, T, D), BF16),
        pltpu.VMEM((2, T, D), F32), pltpu.VMEM((2, 2, T, D), BF16),
        pltpu.VMEM((2, T, 128), F32),
        pltpu.VMEM(slots, BF16), pltpu.VMEM(slots, BF16),
        pltpu.VMEM(slots, BF16), pltpu.VMEM(slots, BF16),
        pltpu.VMEM(slots[1:], BF16), pltpu.VMEM((EXPERTS * SLOTS, D), F32),
        pltpu.VMEM((4, 512, 512), BF16), pltpu.VMEM((4, 512, 512), F32),
        pltpu.VMEM((4, 512, 512), BF16), pltpu.VMEM((T, 3 * D), BF16),
        pltpu.VMEM((4, 2, 512, D), BF16), pltpu.VMEM((2, 2, 2, 512, D), BF16),
        pltpu.VMEM((2, 4, 256, WIDE), BF16), pltpu.VMEM((2, 2, 256, WIDE), BF16),
        pltpu.VMEM((2, 16, 2, 16, WIDE), BF16),
        pltpu.VMEM((2, 2, 16, WIDE), BF16), pltpu.VMEM((4, 16, WIDE), BF16),
        pltpu.VMEM((16, WIDE), BF16),
        pltpu.VMEM((2, T, D), BF16), pltpu.VMEM((2, T, D), BF16),
        pltpu.SemaphoreType.DMA((SEMS,)),
    ]
    lout, lig, up0, up1, dn0, dn1, gd = pl.pallas_call(
        kernel,
        out_shape=(
            jax.ShapeDtypeStruct((2, T, D), BF16),
            jax.ShapeDtypeStruct((2, T, D), BF16),
            jax.ShapeDtypeStruct((2, 512, D), BF16),
            jax.ShapeDtypeStruct((2, 512, D), BF16),
            jax.ShapeDtypeStruct((2, 512, D), BF16),
            jax.ShapeDtypeStruct((2, 512, D), BF16),
            jax.ShapeDtypeStruct((16, 16, WIDE), BF16),
        ),
        in_specs=[vmem, vmem, vmem, anywhere, anywhere, anywhere],
        out_specs=(anywhere,) * 7,
        scratch_shapes=scratch,
        compiler_params=pltpu.CompilerParams(
            has_side_effects=True, collective_id=0, vmem_limit_bytes=63 * 1024 * 1024
        ),
    )(x, cot, rt, shp, up_weight[0], down_weight[0])
    shape_out = (1, 2) + images.shape[1:]
    layer_out = lout[:, :ROWS].reshape(shape_out)
    layer_in_grad = lig[:, :ROWS].reshape(shape_out)
    gathered = gd.reshape(256, WIDE)
    flat = jnp.concatenate([gathered[:128], gathered[128:]], axis=1).astype(F32)
    return (
        layer_out,
        layer_in_grad,
        flat[:, 2080][None],
        flat[:, 0:1536][None],
        flat[:, 1536:2048][None],
        flat[:, 2081][None],
        flat[:, 2048:2080][None],
        (up0.astype(F32) + up1.astype(F32))[None],
        (dn0.astype(F32) + dn1.astype(F32))[None],
    )


def solution(mesh):
    in_specs = (
        P(None, ("expert", "shard"), None, None),
        P(None, ("expert", "shard"), None, None),
        P("section", "shard"),
        P("section", "shard", None),
        P("section", "shard", None),
        P("section", "shard"),
        P("section", "shard", None),
        P("section", "expert", "shard", None),
        P("section", "expert", "shard", None),
        P("section", None, ("expert", "shard"), None, None),
    )
    out_specs = (
        P("section", None, ("expert", "shard"), None, None),
        P("section", None, ("expert", "shard"), None, None),
        P("section", "shard"),
        P("section", "shard", None),
        P("section", "shard", None),
        P("section", "shard"),
        P("section", "shard", None),
        P("section", "expert", "shard", None),
        P("section", "expert", "shard", None),
    )
    return jax.shard_map(shards, mesh=mesh, in_specs=in_specs, out_specs=out_specs, check_vma=False)
```

```python
import jax
import jax.numpy as jnp
from jax import lax
from jax.experimental import pallas as pl
from jax.experimental.pallas import tpu as pltpu
from jax.sharding import PartitionSpec as P

HEADS = 8
HEAD_DIM = 64
TOPK = 2
SEQ = 50
ROWS = 200
T = 256
D = 512
EXPERTS = 32
SLOTS = 16
SHARED = 2176
WIDE = 1152
EPS = 1e-06
F32 = jnp.float32
BF16 = jnp.bfloat16
MESH = pl.DeviceIdType.MESH


def nn(a, b):
    return lax.dot_general(a, b, (((1,), (0,)), ((), ())), preferred_element_type=F32)


def nt(a, b):
    return lax.dot_general(a, b, (((1,), (1,)), ((), ())), preferred_element_type=F32)


def tn(a, b):
    return lax.dot_general(a, b, (((0,), (0,)), ((), ())), preferred_element_type=F32)


def iota(shape, dim):
    return lax.broadcasted_iota(jnp.int32, shape, dim).astype(F32)


def one(condition):
    return jnp.where(condition, 1.0, 0.0)


def normalize(values):
    shifted = values - jnp.mean(values, axis=-1, keepdims=True)
    inverse = lax.rsqrt(jnp.mean(shifted * shifted, axis=-1, keepdims=True) + EPS)
    return shifted * inverse, inverse


def norm_back(grad, normed, inverse):
    mean_grad = jnp.mean(grad, axis=-1, keepdims=True)
    mean_cross = jnp.mean(grad * normed, axis=-1, keepdims=True)
    return inverse * (grad - mean_grad - normed * mean_cross)


ROOT = 0.7978845608028654
CUBE = 0.044715


def gelu(x):
    return 0.5 * x * (1.0 + jnp.tanh(ROOT * (x + CUBE * x * x * x)))


def gelu_both(x):
    square = x * x
    bent = jnp.tanh(ROOT * x * (1.0 + CUBE * square))
    half = 0.5 * (1.0 + bent)
    slope = half + 0.5 * x * (1.0 - bent * bent) * (ROOT * (1.0 + 3.0 * CUBE * square))
    return x * half, slope


A2A_S, A2A_R = 0, 8
ROUTE_S, ROUTE_R = 16, 17
SH_S, SH_R, SHF_S, SHF_R = 18, 19, 21, 23
W_S, W_R, WF_S, WF_R = 25, 26, 28, 30
GWA_S, GWA_R, GWB_S, GWB_R = 32, 36, 40, 44
GSA_S, GSA_R, GSB_S, GSB_R = 46, 48, 50, 52
GSC_S, GSC_R, GSD_S, GSD_R = 54, 58, 59, 60
LO_S, LO_R, LI_S, LI_R = 61, 62, 63, 64
SHX_S, SHX_R = 65, 67
SEMS = 69


def kernel(
    x, cot, rt, shp, up, dn,
    lout, lig, eb_up0, eb_up1, eb_dn0, eb_dn1, gd,
    w, sh, rts, rcol, bias, d_t, p_t,
    qkv_s, o_s, hid, pick, gat,
    rows_b, ret_b, g_b, dr_b, sbuf, acc,
    act_t, gp_t, dp_t, dqkv,
    gw, gwa, gs, gsa, gsb, gsc_s, gsc, gd_s, lo, li, mixed_s, first_s, narrow_s, sem,
):
    s, e, h = lax.axis_index("section"), lax.axis_index("expert"), lax.axis_index("shard")
    zh, c = lax.div(h, 2), lax.rem(h, 2)
    me = e * 2 + s
    sibling = (s, e, 2 * zh + 1 - c)
    other = (1 - s, e, h)

    def put(src, dst, send, recv, device):
        pltpu.make_async_remote_copy(
            src_ref=src, dst_ref=dst, send_sem=sem.at[send], recv_sem=sem.at[recv],
            device_id=device, device_id_type=MESH,
        ).start()

    def local(src, dst, recv):
        pltpu.make_async_copy(src, dst, sem.at[recv]).start()

    def wait(ref, number):
        pltpu.make_async_copy(ref, ref, sem.at[number]).wait()

    def put_or_local(own, src, dst, send, recv, device, here=None):
        @pl.when(own)
        def _():
            local(src, dst, recv if here is None else here)

        @pl.when(jnp.logical_not(own))
        def _():
            put(src, dst, send, recv, device)

    def wait_unless(own, ref, number):
        @pl.when(jnp.logical_not(own))
        def _():
            wait(ref, number)

    def a2a_start(phase, dst):
        local(sbuf.at[me], dst.at[me], A2A_R + phase)

        def step(i, carry):
            t = lax.rem(me + i, EXPERTS)
            put(sbuf.at[t], dst.at[me], A2A_S + phase, A2A_R + phase,
                (lax.rem(t, 2), lax.div(t, 2), h))
            return carry

        lax.fori_loop(1, EXPERTS, step, 0)

    def a2a_finish(phase, dst):
        wait(dst, A2A_R + phase)
        wait(sbuf.at[pl.ds(0, EXPERTS - 1)], A2A_S + phase)

    barrier = pltpu.get_barrier_semaphore()

    def greet(i, carry):
        t = lax.rem(me + i, EXPERTS)
        pl.semaphore_signal(
            barrier, inc=1, device_id=(lax.rem(t, 2), lax.div(t, 2), h), device_id_type=MESH
        )
        return carry

    lax.fori_loop(1, EXPERTS, greet, 0)
    for to_s in range(2):
        for i in range(1, 4):
            pl.semaphore_signal(
                barrier, inc=1, device_id=(to_s, e, lax.rem(h + i, 4)), device_id_type=MESH
            )

    def image_of(index):
        return one(index >= 50) + one(index >= 100) + one(index >= 150) + one(index >= 200)

    bias[...] = jnp.where(
        image_of(iota((T, T), 0)) == image_of(iota((T, T), 1)), 0.0, -1e30
    )
    lane = iota((T, 128), 1)
    first_half = lane < 64.0
    half_row = iota((1, 128), 1)
    halves = (one(half_row < 64.0).astype(BF16), one(half_row >= 64.0).astype(BF16))
    sel_row, sel_lane = iota((8, 128), 0), iota((8, 128), 1)
    select = one(sel_lane == sel_row + 32.0) * one(sel_row < 2.0)
    select = select.astype(BF16)
    rts[s] = rt[s]
    pl.semaphore_wait(barrier, EXPERTS - 1 + 6)

    put(rt.at[1 - s], rts.at[s], ROUTE_S, ROUTE_R, other)
    own_rows = pl.ds(pl.multiple_of(h * 128, 128), 128)
    own_columns = pl.ds(pl.multiple_of(e * 128, 128), 128)
    for layer in range(2):
        @pl.when(s == layer)
        def _():
            for to_s in range(2):
                for to_zh in range(2):
                    for columns in (own_columns, pl.ds(2048, 128)):
                        put_or_local(
                            jnp.logical_and(s == to_s, zh == to_zh),
                            shp.at[:, columns], sh.at[layer, own_rows, columns],
                            SH_S, SH_R + layer, (to_s, e, 2 * to_zh + c),
                        )

    def weights_start(layer, sections):
        @pl.when(s == layer)
        def _():
            for to_s in sections:
                for to_zh in range(2):
                    own = jnp.logical_and(s == to_s, zh == to_zh)
                    device = (to_s, e, 2 * to_zh + c)
                    put_or_local(own, up.at[to_s], w.at[layer, h, 0], W_S, W_R + layer, device)
                    put_or_local(own, dn.at[to_s], w.at[layer, h, 1], W_S, W_R + layer, device)

    weights_start(0, (0, 1))
    weights_start(1, (0, 1))

    def peers(step):
        def body(i, carry):
            step(lax.rem(e + i, 16))
            return carry

        lax.fori_loop(1, 16, body, 0)

    def shared_part(l, from_zh, columns):
        rows = pl.ds(pl.multiple_of((2 * from_zh + c) * 128, 128), 128)
        return sh.at[l, rows, columns]

    def shared_across(l):
        wait(sh.at[l, pl.ds(0, 256), pl.ds(0, 256)], SH_R + l)

        def step(to_e):
            for from_zh in range(2):
                part = shared_part(l, from_zh, own_columns)
                put(part, part, SHX_S + l, SHX_R + l, (s, to_e, h))

        peers(step)

    def shared_forward(l):
        across = sh.at[l, pl.ds(0, 256), pl.ds(0, 1920)]
        wait(across, SHX_R + l)
        for from_zh in range(2):
            part = shared_part(l, from_zh, pl.ds(0, SHARED))
            put(part, part, SHF_S + l, SHF_R + l, sibling)
        wait(sh.at[l, pl.ds(0, 256)], SHF_R + l)
        wait(sh.at[l, pl.ds(0, 256)], SHF_S + l)
        wait(across, SHX_S + l)

    shared_across(0)
    wait(rts.at[0], ROUTE_R)
    wait(rts.at[0], ROUTE_S)
    upper = one(iota((T, T), 0) < iota((T, T), 1)).astype(BF16)
    eye = one(sel_lane == sel_row).astype(BF16)
    for l in range(2):
        route = rts[l]
        number = iota((EXPERTS, T), 0)
        chosen = [one(route[k:k + 1] == number) for k in range(2)]
        earlier = nn((chosen[0] + chosen[1]).astype(BF16), upper)
        slot = [jnp.sum(earlier * chosen[k], axis=0, keepdims=True) for k in range(2)]
        slot_number = iota((EXPERTS * SLOTS, T), 0)
        for k in range(2):
            d_t[l, k] = one(slot_number == route[k:k + 1] * SLOTS + slot[k]).astype(BF16)
        row8 = iota((8, T), 0)
        listing = jnp.where(
            row8 == 0.0, route[0:1],
            jnp.where(row8 == 1.0, route[1:2],
                      jnp.where(row8 == 2.0, slot[0], jnp.where(row8 == 3.0, slot[1], 0.0))),
        )
        columns = tn(listing.astype(BF16), eye)
        rcol[l] = columns
        lane_number = iota((T, EXPERTS * SLOTS), 1)
        for k in range(2):
            target = columns[:, k:k + 1] * SLOTS + columns[:, 2 + k:3 + k]
            p_t[l, k] = one(lane_number == target).astype(BF16)

    def choices(l):
        columns = rcol[l]
        return [one(lane == columns[:, k:k + 1]) for k in range(2)]

    def gains(l):
        rows = nt(select, sh[l, :, 2048:2176])
        return rows[0:1], rows[1:2]

    def weights_forward(l):
        wait(w.at[l, pl.ds(0, 2)], W_R + l)
        for from_zh in range(2):
            part = w.at[l, 2 * from_zh + c]
            put(part, part, WF_S + l, WF_R + l, sibling)

    def weights_finish(l):
        for number in (WF_R + l, WF_S + l):
            wait(w.at[l, pl.ds(0, 2)], number)

    def forward(l):
        rows_in = (x[...] if l == 0 else lo[0]).astype(F32)
        normed, _ = normalize(rows_in)
        shared_forward(l)
        if l == 0:
            shared_across(1)
        gain_one, gain_two = gains(l)
        first_in = (normed * gain_one).astype(BF16)
        qkv_s[l] = nn(first_in, sh[l, :, 0:1536]).astype(BF16)
        for pair in range(4):
            at = pair * 128
            q = qkv_s[l, :, at:at + 128]
            k = qkv_s[l, :, 512 + at:640 + at]
            v = qkv_s[l, :, 1024 + at:1152 + at]
            outs = []
            for half in range(2):
                scores = nt(q * halves[half], k) * (HEAD_DIM ** -0.5) + bias[...]
                raised = jnp.exp(scores - jnp.max(scores, axis=-1, keepdims=True))
                chance = raised / jnp.sum(raised, axis=-1, keepdims=True)
                outs.append(nn(chance.astype(BF16), v))
            o_s[l, :, at:at + 128] = jnp.where(first_half, outs[0], outs[1]).astype(BF16)
        hidden = rows_in + nn(o_s[l], sh[l, :, 1536:2048])
        hid[l] = hidden
        normed, _ = normalize(hidden)
        second_in = (normed * gain_two).astype(BF16)
        sbuf[...] = nn(d_t[l, 0] + d_t[l, 1], second_in).astype(BF16).reshape(EXPERTS, SLOTS, D)
        a2a_start(2 * l, rows_b.at[l])
        logits = nn(second_in, sh[l, :, 2048:2176])
        picked = [jnp.sum(ch * logits, axis=1, keepdims=True) for ch in choices(l)]
        top = jnp.maximum(picked[0], picked[1])
        raised = [jnp.exp(value - top) for value in picked]
        total = raised[0] + raised[1]
        gate = [value / total for value in raised]
        gat[l] = jnp.where(lane == 0.0, gate[0], jnp.where(lane == 1.0, gate[1], 0.0))
        weights_forward(l)
        a2a_finish(2 * l, rows_b.at[l])
        weights_finish(l)
        acc[...] = jnp.zeros_like(acc)

        def piece(j, carry):
            before = nt(rows_b[l].reshape(EXPERTS * SLOTS, D), w[l, j, 0])
            acc[...] += nn(gelu(before).astype(BF16), w[l, j, 1])
            return carry

        lax.fori_loop(0, 4, piece, 0)
        sbuf[...] = acc[...].astype(BF16).reshape(EXPERTS, SLOTS, D)
        a2a_start(2 * l + 1, ret_b.at[l])
        a2a_finish(2 * l + 1, ret_b.at[l])
        returned = ret_b[l].reshape(EXPERTS * SLOTS, D)
        result = hid[l]
        for k in range(2):
            mine = nn(p_t[l, k], returned)
            pick[l, k] = mine.astype(BF16)
            result = result + gat[l, :, k:k + 1] * mine
        lo[l] = result.astype(BF16)

    def gw_a(l, to_zh):
        number = 2 * l + to_zh
        put(gw.at[2 * to_zh + 1 - c], gwa.at[l, to_zh], GWA_S + number, GWA_R + number, sibling)

    def gw_b(l):
        for to_zh in range(2):
            j = 2 * to_zh + c
            number = 2 * l + to_zh
            own = jnp.logical_and(s == l, zh == to_zh)
            wait(gwa.at[l, to_zh], GWA_R + number)
            gw[j] = (gw[j].astype(F32) + gwa[l, to_zh].astype(F32)).astype(BF16)
            send = GWB_S + number
            for from_zh, outs in enumerate(((eb_up0, eb_dn0), (eb_up1, eb_dn1))):
                @pl.when(zh == from_zh)
                def _():
                    for u in range(2):
                        put_or_local(own, gw.at[j, u], outs[u].at[s], send, GWB_R, (l, e, j), send)

    def gw_sent(l):
        for to_zh in range(2):
            wait(gwa.at[l, to_zh], GWA_S + 2 * l + to_zh)
            wait(gw.at[0], GWB_S + 2 * l + to_zh)

    def gs_a(l):
        for to_zh in range(2):
            put(gs.at[l, 2 * to_zh + 1 - c], gsa.at[l, to_zh], GSA_S + l, GSA_R + l, sibling)

    def gs_b(l):
        wait(gsa.at[l], GSA_R + l)
        for to_zh in range(2):
            j = 2 * to_zh + c
            gs[l, j] = (gs[l, j].astype(F32) + gsa[l, to_zh].astype(F32)).astype(BF16)

        def part(to_zh, to_e):
            return gs.at[l, 2 * to_zh + c, pl.ds(pl.multiple_of(to_e * 16, 16), 16)]

        def step(to_e):
            for to_zh in range(2):
                put(part(to_zh, to_e), gsb.at[l, e, to_zh], GSB_S + l, GSB_R + l, (s, to_e, h))

        for to_zh in range(2):
            local(part(to_zh, e), gsb.at[l, e, to_zh], GSB_R + l)
        peers(step)

    def gs_c(l):
        wait(gsb.at[l], GSB_R + l)
        total = gsb[l, 0].astype(F32)
        for source in range(1, 16):
            total = total + gsb[l, source].astype(F32)
        gsc_s[l] = total.astype(BF16)
        for to_zh in range(2):
            own = jnp.logical_and(s == l, zh == to_zh)
            put_or_local(own, gsc_s.at[l, to_zh], gsc.at[2 * s + zh], GSC_S + 2 * l + to_zh, GSC_R,
                         (l, e, 2 * to_zh + c))

    def gs_d():
        wait(gsc, GSC_R)
        total = gsc[0].astype(F32)
        for source in range(1, 4):
            total = total + gsc[source].astype(F32)
        gd_s[...] = total.astype(BF16)
        local(gd_s, gd.at[e], GSD_R)
        peers(lambda to_e: put(gd_s, gd.at[e], GSD_S, GSD_R, (s, to_e, h)))

    def gs_sent(l):
        wait(gsa.at[l], GSA_S + l)
        wait(gsb.at[l, pl.ds(0, 15)], GSB_S + l)
        for to_zh in range(2):
            wait_unless(jnp.logical_and(s == l, zh == to_zh), gsc_s.at[l, to_zh], GSC_S + 2 * l + to_zh)

    def shared_grads(l):
        for j in range(4):
            at = slice(j * 128, (j + 1) * 128)
            part = tn(first_s[:, at], dqkv[...]).astype(BF16)
            gs[l, j, 0:128, :] = part[:, 0:WIDE]
            gs[l, j, 128:256, 0:384] = part[:, WIDE:1536]
            gs[l, j, 128:256, 384:896] = tn(o_s[l, :, at], mixed_s[...]).astype(BF16)
            gs[l, j, 128:256, 896:1024] = narrow_s[at]
            gs[l, j, 128:256, 1024:1152] = jnp.zeros((128, 128), BF16)
        gs_a(l)

    def backward(l, grad_out, hook_one, hook_two):
        gate = [gat[l, :, k:k + 1] for k in range(2)]
        grad_gate = [
            jnp.sum(grad_out * pick[l, k].astype(F32), axis=-1, keepdims=True) for k in range(2)
        ]
        copies = [(gate[k] * grad_out).astype(BF16) for k in range(2)]
        sent = nn(d_t[l, 0], copies[0]) + nn(d_t[l, 1], copies[1])
        sbuf[...] = sent.astype(BF16).reshape(EXPERTS, SLOTS, D)
        a2a_start(4 + 2 * l, g_b.at[l])

        def again(j, carry):
            before = nt(w[l, j, 0], rows_b[l].reshape(EXPERTS * SLOTS, D))
            active, slope = gelu_both(before)
            act_t[j] = active.astype(BF16)
            gp_t[j] = slope
            return carry

        lax.fori_loop(0, 4, again, 0)
        hook_one()
        a2a_finish(4 + 2 * l, g_b.at[l])
        acc[...] = jnp.zeros_like(acc)

        def back(j, carry):
            grad_active = nt(w[l, j, 1], g_b[l].reshape(EXPERTS * SLOTS, D))
            grad_before = (grad_active * gp_t[j]).astype(BF16)
            dp_t[j] = grad_before
            acc[...] += tn(grad_before, w[l, j, 0])
            return carry

        lax.fori_loop(0, 4, back, 0)
        sbuf[...] = acc[...].astype(BF16).reshape(EXPERTS, SLOTS, D)
        a2a_start(5 + 2 * l, dr_b.at[l])

        def weight_grads(i, carry):
            j = 2 * lax.rem(i, 2) + jnp.where(i < 2, 1 - c, c)
            gw[j, 1] = nn(act_t[j], g_b[l].reshape(EXPERTS * SLOTS, D)).astype(BF16)
            gw[j, 0] = nn(dp_t[j], rows_b[l].reshape(EXPERTS * SLOTS, D)).astype(BF16)
            for to_zh in range(2):
                @pl.when(i == to_zh)
                def _():
                    gw_a(l, to_zh)
            return carry

        if l == 0:
            gw_sent(1)
        lax.fori_loop(0, 4, weight_grads, 0)
        total = gate[0] * grad_gate[0] + gate[1] * grad_gate[1]
        chosen = choices(l)
        grad_logits = (
            chosen[0] * (gate[0] * (grad_gate[0] - total))
            + chosen[1] * (gate[1] * (grad_gate[1] - total))
        ).astype(BF16)
        gw_b(l)
        a2a_finish(5 + 2 * l, dr_b.at[l])
        hook_two()
        gain_one, gain_two = gains(l)
        returned = dr_b[l].reshape(EXPERTS * SLOTS, D)
        grad_second = nn(p_t[l, 0] + p_t[l, 1], returned) + nt(grad_logits, sh[l, :, 2048:2176])
        normed, inverse = normalize(hid[l])
        second_in = (normed * gain_two).astype(BF16)
        gain_two_grad = jnp.sum(grad_second * normed, axis=0, keepdims=True)
        grad_hidden = grad_out + norm_back(grad_second * gain_two, normed, inverse)
        grad_mixed = grad_hidden.astype(BF16)
        router_grad = tn(second_in, grad_logits)
        grad_heads = nt(grad_mixed, sh[l, :, 1536:2048]).astype(BF16)
        mixed_s[...] = grad_mixed
        for pair in range(4):
            at = pair * 128
            q = qkv_s[l, :, at:at + 128]
            k = qkv_s[l, :, 512 + at:640 + at]
            v = qkv_s[l, :, 1024 + at:1152 + at]
            do = grad_heads[:, at:at + 128]
            grads = []
            for half in range(2):
                scores = nt(k, q * halves[half]) * (HEAD_DIM ** -0.5) + bias[...]
                raised = jnp.exp(scores - jnp.max(scores, axis=0, keepdims=True))
                chance = raised / jnp.sum(raised, axis=0, keepdims=True)
                grad_value = nn(chance.astype(BF16), do)
                grad_chance = nt(v, do * halves[half])
                cross = jnp.sum(chance * grad_chance, axis=0, keepdims=True)
                grad_scores = (chance * (grad_chance - cross)).astype(BF16)
                grad_key = nn(grad_scores, q) * (HEAD_DIM ** -0.5)
                grad_query = tn(grad_scores, k) * (HEAD_DIM ** -0.5)
                grads.append((grad_query, grad_key, grad_value))
            for part in range(3):
                both = jnp.where(first_half, grads[0][part], grads[1][part])
                dqkv[:, part * 512 + at:part * 512 + at + 128] = both.astype(BF16)
        rows_in = (x[...] if l == 0 else lo[0]).astype(F32)
        normed, inverse = normalize(rows_in)
        first_in = (normed * gain_one).astype(BF16)
        grad_first = nt(dqkv[...], sh[l, :, 0:1536])
        gain_one_grad = jnp.sum(grad_first * normed, axis=0, keepdims=True)
        grad_in = grad_hidden + norm_back(grad_first * gain_one, normed, inverse)
        li[l] = grad_in.astype(BF16)
        row8 = iota((8, D), 0)
        both = jnp.where(row8 == 0.0, gain_one_grad, jnp.where(row8 == 1.0, gain_two_grad, 0.0))
        narrow_s[...] = (router_grad + tn(both.astype(BF16), select)).astype(BF16)
        first_s[...] = first_in

    def exchange(mine, out, send, recv):
        local(mine.at[s], out.at[s], recv)
        put(mine.at[1 - s], out.at[s], send, recv, other)

    def nothing():
        return None

    forward(0)
    forward(1)
    exchange(lo, lout, LO_S, LO_R)
    backward(1, cot[...].astype(F32), nothing, nothing)

    def first_hook():
        shared_grads(1)

    def second_hook():
        gs_b(1)

    backward(0, li[1].astype(F32), first_hook, second_hook)
    shared_grads(0)
    exchange(li, lig, LI_S, LI_R)
    gs_c(1)
    gs_b(0)
    gs_c(0)
    gs_d()
    gw_sent(0)
    gs_sent(1)
    gs_sent(0)
    wait(sh.at[0, pl.ds(0, 384), pl.ds(0, 256)], SH_S)
    wait(w.at[0, pl.ds(0, 3)], W_S)
    wait(gd.at[pl.ds(0, 15)], GSD_S)
    wait(gd, GSD_R)
    for out, send, recv in ((lout, LO_S, LO_R), (lig, LI_S, LI_R)):
        wait(out, recv)
        wait(out.at[0], send)
    wait(gw.at[pl.ds(0, 3)], GWB_R)


def shards(
    images, cotangent, ln1_gain, qkv_weight, out_weight, ln2_gain, router_weight,
    up_weight, down_weight, routes,
):
    section = lax.axis_index("section")
    pad = ((0, T - ROWS), (0, 0))
    x = jnp.pad(lax.dynamic_index_in_dim(images, section, 0, False).reshape(ROWS, D), pad)
    cot = jnp.pad(lax.dynamic_index_in_dim(cotangent, section, 0, False).reshape(ROWS, D), pad)
    rt = jnp.swapaxes(routes[0].reshape(2, ROWS, TOPK), 1, 2).astype(F32)
    rt = jnp.pad(rt, ((0, 0), (0, 6), (0, T - ROWS)), constant_values=-1.0)
    shp = jnp.concatenate(
        [qkv_weight[0], out_weight[0], router_weight[0], ln1_gain[0][:, None],
         ln2_gain[0][:, None], jnp.zeros((128, 94), BF16)], axis=1,
    )
    vmem, anywhere = pl.BlockSpec(memory_space=pltpu.VMEM), pl.BlockSpec(memory_space=pl.ANY)
    slots = (2, EXPERTS, SLOTS, D)
    scratch = [
        pltpu.VMEM((2, 4, 2, 512, D), BF16),
        pltpu.VMEM((2, D, SHARED), BF16),
        pltpu.VMEM((2, 8, T), F32), pltpu.VMEM((2, T, 128), F32),
        pltpu.VMEM((T, T), F32),
        pltpu.VMEM((2, 2, EXPERTS * SLOTS, T), BF16), pltpu.VMEM((2, 2, T, EXPERTS * SLOTS), BF16),
        pltpu.VMEM((2, T, 3 * D), BF16), pltpu.VMEM((2, T, D), BF16),
        pltpu.VMEM((2, T, D), F32), pltpu.VMEM((2, 2, T, D), BF16),
        pltpu.VMEM((2, T, 128), F32),
        pltpu.VMEM(slots, BF16), pltpu.VMEM(slots, BF16),
        pltpu.VMEM(slots, BF16), pltpu.VMEM(slots, BF16),
        pltpu.VMEM(slots[1:], BF16), pltpu.VMEM((EXPERTS * SLOTS, D), F32),
        pltpu.VMEM((4, 512, 512), BF16), pltpu.VMEM((4, 512, 512), F32),
        pltpu.VMEM((4, 512, 512), BF16), pltpu.VMEM((T, 3 * D), BF16),
        pltpu.VMEM((4, 2, 512, D), BF16), pltpu.VMEM((2, 2, 2, 512, D), BF16),
        pltpu.VMEM((2, 4, 256, WIDE), BF16), pltpu.VMEM((2, 2, 256, WIDE), BF16),
        pltpu.VMEM((2, 16, 2, 16, WIDE), BF16),
        pltpu.VMEM((2, 2, 16, WIDE), BF16), pltpu.VMEM((4, 16, WIDE), BF16),
        pltpu.VMEM((16, WIDE), BF16),
        pltpu.VMEM((2, T, D), BF16), pltpu.VMEM((2, T, D), BF16),
        pltpu.VMEM((T, D), BF16), pltpu.VMEM((T, D), BF16),
        pltpu.VMEM((D, 128), BF16),
        pltpu.SemaphoreType.DMA((SEMS,)),
    ]
    lout, lig, up0, up1, dn0, dn1, gd = pl.pallas_call(
        kernel,
        out_shape=(
            jax.ShapeDtypeStruct((2, T, D), BF16),
            jax.ShapeDtypeStruct((2, T, D), BF16),
            jax.ShapeDtypeStruct((2, 512, D), BF16),
            jax.ShapeDtypeStruct((2, 512, D), BF16),
            jax.ShapeDtypeStruct((2, 512, D), BF16),
            jax.ShapeDtypeStruct((2, 512, D), BF16),
            jax.ShapeDtypeStruct((16, 16, WIDE), BF16),
        ),
        in_specs=[vmem, vmem, vmem, anywhere, anywhere, anywhere],
        out_specs=(anywhere,) * 7,
        scratch_shapes=scratch,
        compiler_params=pltpu.CompilerParams(
            has_side_effects=True, collective_id=0, vmem_limit_bytes=63 * 1024 * 1024
        ),
    )(x, cot, rt, shp, up_weight[0], down_weight[0])
    shape_out = (1, 2) + images.shape[1:]
    layer_out = lout[:, :ROWS].reshape(shape_out)
    layer_in_grad = lig[:, :ROWS].reshape(shape_out)
    gathered = gd.reshape(256, WIDE)
    flat = jnp.concatenate([gathered[:128], gathered[128:]], axis=1).astype(F32)
    return (
        layer_out,
        layer_in_grad,
        flat[:, 2080][None],
        flat[:, 0:1536][None],
        flat[:, 1536:2048][None],
        flat[:, 2081][None],
        flat[:, 2048:2080][None],
        (up0.astype(F32) + up1.astype(F32))[None],
        (dn0.astype(F32) + dn1.astype(F32))[None],
    )


def solution(mesh):
    in_specs = (
        P(None, ("expert", "shard"), None, None),
        P(None, ("expert", "shard"), None, None),
        P("section", "shard"),
        P("section", "shard", None),
        P("section", "shard", None),
        P("section", "shard"),
        P("section", "shard", None),
        P("section", "expert", "shard", None),
        P("section", "expert", "shard", None),
        P("section", None, ("expert", "shard"), None, None),
    )
    out_specs = (
        P("section", None, ("expert", "shard"), None, None),
        P("section", None, ("expert", "shard"), None, None),
        P("section", "shard"),
        P("section", "shard", None),
        P("section", "shard", None),
        P("section", "shard"),
        P("section", "shard", None),
        P("section", "expert", "shard", None),
        P("section", "expert", "shard", None),
    )
    return jax.shard_map(shards, mesh=mesh, in_specs=in_specs, out_specs=out_specs, check_vma=False)
```
